512 devices in a mesh: tower: 16 (over y, core), shard: 32 (over z, x).
Axes of the slice: x: 4, y: 8, z: 8, core: 2. Of those that a mesh axis runs over, the one named last changes fastest.
Arguments:
- out_grad: bfloat16 [4096, 16, 256], P(('tower', 'shard')), may hold values from -6 to 6
- hidden_pre: bfloat16 [16, 4096, 1024], P('tower', 'shard'), may hold values from -6 to 6
- down_proj: bfloat16 [16, 1024, 256], P('tower'), may hold values from -0.1875 to 0.1875
- up_proj: bfloat16 [16, 4096, 1024], P('tower'), may hold values from -0.09375 to 0.09375
- feature_slot: int32 [16, 32], P('tower'), may hold values from 0 to 31, each once within a row
- element_segment: int32 [16, 32, 5120], P('tower', 'shard'), may hold values from 0 to 4095, never falling along the last dimension, each value on 1 to 4 neighbouring positions
- element_weight: float32 [16, 32, 5120], P('tower', 'shard'), may hold values from 0.25 to 1.75
- row_owner: int32 [16, 32, 5120, 1], P('tower', 'shard'), may hold values from 0 to 31; in each aligned block of 5120 rows (0 to 5119, 5120 to 10239, ..., all dimensions but the last counted through in order) at most 320 rows name the same one
- row_local: int32 [16, 32, 5120], P('tower', 'shard'), may hold values from 0 to 511
Outputs:
- table_grad: float32 [16, 16384, 128], P('tower', 'shard')
The draws below stay inside these ranges and needn't reach their ends.
Inputs may be any that keep to these rules, and one draw needn't show every extreme that they name: `element_segment`: segment c of a device is the jagged sequence of its sample c // 32 and feature c % 32; numbers never fall along a device's elements, each of the 4096 segments holds 1 to 4 elements and some holds 4. `row_owner`: among the 5120 elements of one device no shard is named more than 320 times, a bound that some block reaches. `feature_slot`: each tower's slots name every block once.
All inputs are finite; a program needn't handle non-finite values.
Results may differ from the reference program's by a relative error of at most 0.005.
Values may be sent and summed in bfloat16 or wider, within the bound.
No kernel may reach another device: no remote copies, remote signals or barrier semaphores. Data moves between devices by JAX's collectives and lax.ppermute only.
A program may use at most 64 MiB of HBM per device.

```python
import math
import jax
import jax.numpy as jnp
import numpy as np
from jax import lax

E = 128
FEAT = 32
HID = 1024
TOUT = 256
MAXLEN = 4
SAMP_DEV = 8
ROW_DEV = 512
TOWERS = 16
SHARDS = 32
TIN = 4096
ROWS_T = 128
SAMPLES = 4096
ELEM_DEV = 5120
CAP = 320
TABLE_ROWS = 16384
N_TOWER = 16
N_SHARD = 32


def set_ends(entries, own_key, smallest, high):
    longest = entries.shape.index(max(entries.shape))
    spots = []
    for shift in (0, 1):
        where = [jax.random.randint(jax.random.fold_in(own_key, axis), (), 0, length) for axis, length in enumerate(entries.shape)]
        where[longest] = (where[longest] + shift) % entries.shape[longest]
        spots.append(tuple(where))
    return entries.at[spots[0]].set(smallest).at[spots[1]].set(high)


def block_scale(rng, extent, pieces, low, high):
    def one(dim, blocks):
        heights = jax.random.uniform(jax.random.fold_in(jax.random.fold_in(rng, 6), dim), (blocks,), jnp.float32, low / len(pieces), high / len(pieces))
        return jnp.repeat(jnp.exp(heights), extent[dim] // blocks).reshape((-1,) + (1,) * (len(extent) - dim - 1))

    loudness = one(*pieces[0])
    for cut in pieces[1:]:
        loudness = loudness * one(*cut)
    return loudness


def rank_table(amount, lean):
    portions = [(1 << 20) // math.isqrt(grade ** lean) + 1 for grade in range(1, amount + 1)]
    spread = 1 + sum(portions) // (1 << 30)
    return np.cumsum(np.array([max(1, weight // spread) for weight in portions]))


def ranked(key, shape, amount, lean):
    grid = rank_table(amount, lean)
    ticket = jax.random.randint(jax.random.fold_in(key, 1), shape, 0, int(grid[amount - 1]))
    grade = jnp.searchsorted(jnp.asarray(grid, jnp.int32), ticket, side="right")
    return jax.random.permutation(jax.random.fold_in(key, 2), amount)[grade].astype(jnp.int32)


def profile(count, total, bound, lean):
    weights = [(1 << 20) // math.isqrt(rank ** lean) + 1 for rank in range(2, count + 1)]
    spare, given = total - bound - (count - 1), [1] * (count - 1)
    while spare > 0:
        free = [i for i in range(count - 1) if given[i] < bound]
        mass, budget = sum([weights[i] for i in free]), spare
        for i in free:
            addition = min(bound - given[i], max(1, budget * weights[i] // mass), spare)
            given[i] = given[i] + addition
            spare = spare - addition
    return np.array([bound] + given)


def ragged_sizes(rng, number_of, total, limit, lean):
    if number_of == 2:
        one = jax.random.randint(rng, (), max(1, total - limit), min(limit, total - 1) + 1)
        return jnp.stack([one, total - one])
    sizes = jnp.asarray(profile(number_of, total, limit, lean), jnp.int32)
    couples = (number_of - 1) // 2
    giver, sink = sizes[1:1 + 2 * couples:2], sizes[2:2 + 2 * couples:2]
    slack = jnp.minimum(giver - 1, limit - sink)
    moved = jax.random.randint(jax.random.fold_in(rng, 1), (couples,), 0, 1 << 20) % (slack + 1)
    sizes = sizes.at[1:1 + 2 * couples:2].set(giver - moved).at[2:2 + 2 * couples:2].set(sink + moved)
    return sizes[jax.random.permutation(jax.random.fold_in(rng, 2), number_of)]


def routed_block(own_key, own, number, rows, amount, top, limit, lean):
    order = jax.random.permutation(own_key, amount)
    packed, usual = load_shares(amount, rows * top, limit, lean, True), load_shares(amount, rows * top, limit, lean, False)
    places = jnp.arange(amount)

    def named(lengths, offset_by):
        used = int((lengths > 0).sum())
        fixed = max(1, used // 4)
        moved = fixed + (places - fixed + offset_by * (used - fixed)) % max(1, amount - fixed)
        return jnp.zeros((amount,), jnp.int32).at[order[jnp.where(places < fixed, places, moved)]].set(jnp.asarray(lengths, jnp.int32))

    lengths = jnp.where(number % 4 == 0, named(packed, number // 4), named(usual, number - number // 4 - 1))
    mixed = jax.random.permutation(jax.random.fold_in(own, 3), amount)
    source_of, receiver = mixed[0:amount // 2 * 2:2], mixed[1:amount // 2 * 2:2]
    slack = jnp.minimum(lengths[source_of] - 1, limit - lengths[receiver]) // 2
    slack = jnp.where((source_of == order[0]) | (receiver == order[0]) | (lengths[receiver] == 0), 0, jnp.maximum(slack, 0))
    moved = jax.random.randint(jax.random.fold_in(own, 4), (amount // 2,), 0, 1 << 20) % (slack + 1)
    lengths = lengths.at[source_of].add(-moved).at[receiver].add(moved)
    items = jnp.searchsorted(jnp.cumsum(lengths), jnp.arange(rows * top), side="right").astype(jnp.int32)
    listing = items.reshape(top, rows).T
    listing = listing[jax.random.permutation(jax.random.fold_in(own, 1), rows)]
    offset_by = jax.random.randint(jax.random.fold_in(own, 2), (rows, 1), 0, top)
    return jnp.take_along_axis(listing, (jnp.arange(top)[None, :] + offset_by) % top, axis=1)


def load_shares(amount, total, bound, lean, full):
    loads = [(1 << 20) // math.isqrt(grade ** lean) + 1 for grade in range(1, amount + 1)]
    largest = bound if full else min(bound, max(-(-total // amount), total * loads[0] // sum(loads)))
    least = 1 if total - largest >= amount - 1 else 0
    given, rest = [largest] + [least] * (amount - 1), total - largest - least * (amount - 1)
    while rest > 0:
        free = [i for i in range(1, amount) if given[i] < largest] or [i for i in range(1, amount) if given[i] < bound]
        pool, remaining = sum([loads[i] for i in free]), rest
        for i in free:
            more = min(bound - given[i], max(1, remaining * loads[i] // pool), rest)
            given[i] = given[i] + more
            rest = rest - more
    return np.array(given)


def normal_values(rng, dims, scale, reach, shards=(), kind=jnp.bfloat16):
    entries = jax.random.normal(rng, dims, jnp.float32) * scale
    if len(shards) > 0:
        entries = block_scale(rng, dims, shards, -0.22, 0.18) * entries
    return jnp.clip(entries, min=-reach, max=reach).astype(kind)


def setup_inputs(seed: int = 0) -> dict:
    key_list = jax.random.split(jax.random.key(seed), 10)
    out_grad = normal_values(key_list[0], (SAMPLES, TOWERS, TOUT), 1.0, 6.0, ((0, 512),))
    hidden_pre = normal_values(key_list[1], (TOWERS, SAMPLES, HID), 1.0, 6.0, ((0, 16), (1, 32)))
    down_proj = normal_values(key_list[2], (TOWERS, HID, TOUT), HID ** -0.5, 0.1875, ((0, 16),))
    up_proj = normal_values(key_list[3], (TOWERS, TIN, HID), TIN ** -0.5, 0.09375, ((0, 16),))
    feature_slot = jax.vmap(lambda own: jax.random.permutation(own, FEAT))(jax.random.split(key_list[4], TOWERS)).reshape((TOWERS, FEAT)).astype(jnp.int32)
    element_segment = jax.vmap(lambda own: jnp.searchsorted(jnp.cumsum(ragged_sizes(own, ROWS_T * FEAT, ELEM_DEV, MAXLEN, 0)), jnp.arange(ELEM_DEV), side="right"))(jax.random.split(key_list[5], TOWERS * SHARDS)).reshape((TOWERS, SHARDS, ELEM_DEV)).astype(jnp.int32)
    element_weight = jnp.clip(0.25 + 1.5 * jax.random.uniform(key_list[6], (TOWERS, SHARDS, ELEM_DEV), jnp.float32) ** block_scale(key_list[6], (TOWERS, SHARDS, ELEM_DEV), ((0, 16), (1, 32)), -0.2, 0.2), 0.25, 1.75)
    row_owner_keys = jax.random.split(jax.random.fold_in(key_list[7], 1), TOWERS * SHARDS * ELEM_DEV // ELEM_DEV)
    row_owner_turns = jax.random.permutation(jax.random.fold_in(key_list[7], 3), TOWERS * SHARDS * ELEM_DEV // ELEM_DEV)
    row_owner = jax.vmap(lambda own, number: routed_block(jax.random.fold_in(key_list[7], 2), own, number, ELEM_DEV, SHARDS, 1, CAP, 1))(row_owner_keys, row_owner_turns).reshape((TOWERS, SHARDS, ELEM_DEV, 1))
    row_local = set_ends(ranked(key_list[8], (TOWERS, SHARDS, ELEM_DEV), ROW_DEV, 1), jax.random.fold_in(key_list[8], 3), 0, ROW_DEV - 1).astype(jnp.int32)
    return {"out_grad": out_grad, "hidden_pre": hidden_pre, "down_proj": down_proj, "up_proj": up_proj, "feature_slot": feature_slot, "element_segment": element_segment, "element_weight": element_weight, "row_owner": row_owner, "row_local": row_local}


def reference(out_grad, hidden_pre, down_proj, up_proj, feature_slot, element_segment, element_weight, row_owner, row_local):
    regrouped = out_grad.reshape(N_TOWER, N_SHARD, SAMP_DEV, TOWERS, TOUT)
    regrouped = jnp.transpose(regrouped, (3, 1, 0, 2, 4)).reshape(TOWERS, SAMPLES, TOUT)
    shard_base = (jnp.arange(N_SHARD, dtype=jnp.int32) * ROWS_T)[:, None]

    def one_tower(operands):
        grad_rows, hidden, w_down, w_up, slots, segment, weights, owner_shard, local_rows = operands
        backward = jnp.dot(grad_rows, w_down.T, preferred_element_type=jnp.float32)
        hid_grad = jnp.where(hidden > 0, backward, 0.0).astype(jnp.bfloat16)
        pooled = jnp.dot(hid_grad, w_up.T, preferred_element_type=jnp.float32).astype(jnp.bfloat16)
        pooled_flat = pooled.reshape(SAMPLES * FEAT, E)
        row_index = (segment // FEAT + shard_base).astype(jnp.int32)
        slot_index = slots[segment % FEAT].astype(jnp.int32)
        gathered = pooled_flat[row_index * FEAT + slot_index]
        elem_grads = (gathered.astype(jnp.float32) * weights[..., None]).astype(jnp.bfloat16)
        global_row = (owner_shard[..., 0] * ROW_DEV + local_rows).astype(jnp.int32)
        table_grad = jnp.zeros((TABLE_ROWS, E), jnp.float32)
        return table_grad.at[global_row.reshape(-1)].add(elem_grads.reshape(-1, E).astype(jnp.float32))

    return lax.map(one_tower, (regrouped, hidden_pre, down_proj, up_proj, feature_slot, element_segment, element_weight, row_owner, row_local))
```

```python
import functools

import jax
import jax.numpy as jnp
from jax import lax
from jax.experimental import pallas as pl
from jax.experimental.pallas import tpu as pltpu
from jax.sharding import Mesh
from jax.sharding import PartitionSpec as P

E = 128
FEAT = 32
SAMP = 128
HID = 1024
TOUT = 256
TIN = 4096
ROW_DEV = 512
ELEMS = 5120
CAP = 320
NX = 4
NZ = 8
HALVES = 2
HALF = ROW_DEV // HALVES
BUCKETS = NZ * HALVES
SUBS = NX * BUCKETS
PIECES = 6
SLOTS = 384
LANES = 128
CHUNKS = SLOTS // LANES
STEP = 512
UNROLL = 16
BF = jnp.bfloat16
F32 = jnp.float32
I32 = jnp.int32
NT = (((1,), (1,)), ((), ()))


def bucket_kernel(seg_ref, weight_ref, owner_ref, row_ref, slot_ref, out_ref, acc_ref):
    upper = (
        lax.broadcasted_iota(I32, (STEP, STEP), 0) <= lax.broadcasted_iota(I32, (STEP, STEP), 1)
    ).astype(F32).astype(BF)
    sub_ids = lax.broadcasted_iota(I32, (SUBS, STEP), 0)
    feat_ids = lax.broadcasted_iota(I32, (FEAT, STEP), 0)
    slot_ids = lax.broadcasted_iota(I32, (SLOTS, STEP), 0).astype(F32)
    acc_ref[...] = jnp.zeros_like(acc_ref)

    def step(k, carry):
        cols = pl.ds(pl.multiple_of(k * STEP, STEP), STEP)
        seg = seg_ref[:, cols]
        weight = weight_ref[:, cols]
        owner = owner_ref[:, cols]
        row = row_ref[:, cols]
        sub = (owner & 3) * BUCKETS + (row >> 8) * NZ + (owner >> 2)
        mine = sub_ids == sub
        ones = jnp.where(mine, 1.0, 0.0)
        inclusive = jnp.dot(ones.astype(BF), upper, preferred_element_type=F32) + carry
        rank = jnp.sum(ones * inclusive, axis=0, keepdims=True) - 1.0
        block = jnp.sum(
            jnp.where(feat_ids == (seg & 31), slot_ref[...], 0.0), axis=0, keepdims=True
        )
        sample = (seg >> 5).astype(F32)
        row_next = ((row & 255) + 1).astype(F32)
        high = weight.astype(BF).astype(F32)
        rest = weight - high
        middle = rest.astype(BF).astype(F32)
        low = rest - middle
        pieces = (block, sample, row_next, high, middle, low)
        left = jnp.concatenate([(ones * piece).astype(BF) for piece in pieces], axis=0)
        right = jnp.where(slot_ids == rank, 1.0, 0.0).astype(BF)
        acc_ref[...] += lax.dot_general(left, right, NT, preferred_element_type=F32)
        return inclusive[:, STEP - 1 : STEP]

    count = lax.fori_loop(0, ELEMS // STEP, step, jnp.zeros((SUBS, 1), F32))
    count = jnp.broadcast_to(count.astype(I32), (SUBS, LANES))
    count_parts = ((count >> 7).astype(F32), (count & 127).astype(F32))
    spare = lax.broadcasted_iota(I32, (SUBS, LANES), 1) >= CAP - (CHUNKS - 1) * LANES
    for p in range(PIECES):
        for c in range(CHUNKS):
            part = acc_ref[p * SUBS : (p + 1) * SUBS, c * LANES : (c + 1) * LANES]
            if p < 2 and c == CHUNKS - 1:
                part = jnp.where(spare, count_parts[p], part)
            part = part.astype(BF)
            for x in range(NX):
                out_ref[x, p, c] = part[x * BUCKETS : (x + 1) * BUCKETS]


def bucket_elements(segment, weight, owner, row, slots):
    return pl.pallas_call(
        bucket_kernel,
        out_shape=jax.ShapeDtypeStruct((NX, PIECES, CHUNKS, BUCKETS, LANES), BF),
        in_specs=[pl.BlockSpec(memory_space=pltpu.VMEM)] * 5,
        out_specs=pl.BlockSpec(memory_space=pltpu.VMEM),
        scratch_shapes=[pltpu.VMEM((PIECES * SUBS, SLOTS), F32)],
        compiler_params=pltpu.CompilerParams(vmem_limit_bytes=32 << 20),
        cost_estimate=pl.CostEstimate(flops=3 << 30, bytes_accessed=1 << 20, transcendentals=0),
    )(segment, weight, owner, row, slots)


def add_elements(half, index_ref, weight_ref, row_ref, pooled_ref, group_ref, total_ref, out_ref):
    group_ref[...] = jnp.zeros_like(group_ref)

    def fetch(x, place, count):
        def some(i, unused):
            base = pl.multiple_of(i * UNROLL, UNROLL)
            for u in range(UNROLL):
                source = index_ref[place, base + u] + x * (FEAT * SAMP)
                scale = weight_ref[place, base + u]
                value = pooled_ref[pl.ds(source, 1), :] * scale
                group_ref[pl.ds(x * LANES + base + u, 1), :] = value
            return unused

        lax.fori_loop(0, (count + (UNROLL - 1)) // UNROLL, some, 0)

    def owner_step(o, unused):
        bucket = half * NZ + o
        places = [x * CHUNKS * BUCKETS + bucket for x in range(NX)]
        counts = [
            index_ref[places[x] + (CHUNKS - 1) * BUCKETS, CAP - (CHUNKS - 1) * LANES]
            for x in range(NX)
        ]
        for x in range(NX):
            fetch(x, places[x], jnp.minimum(counts[x], LANES))
        rows = jnp.concatenate([row_ref[pl.ds(places[x], 1), :] for x in range(NX)], axis=1)
        row_ids = lax.broadcasted_iota(I32, (HALF, NX * LANES), 0) + 1
        chosen = jnp.where(row_ids == rows, 1.0, 0.0).astype(BF)
        total_ref[...] = jnp.dot(
            chosen, group_ref[...].astype(BF), preferred_element_type=F32
        )
        for x in range(NX):
            for c in range(1, CHUNKS):

                @pl.when(counts[x] > c * LANES)
                def _():
                    place = places[x] + c * BUCKETS
                    fetch(x, place, jnp.minimum(counts[x] - c * LANES, LANES))
                    ids = lax.broadcasted_iota(I32, (HALF, LANES), 0) + 1
                    more = jnp.where(ids == row_ref[pl.ds(place, 1), :], 1.0, 0.0).astype(BF)
                    total_ref[...] += jnp.dot(
                        more,
                        group_ref[x * LANES : (x + 1) * LANES, :].astype(BF),
                        preferred_element_type=F32,
                    )

        out_ref[o] = total_ref[...].astype(BF)
        return unused

    lax.fori_loop(0, NZ, owner_step, 0)


UP_STEP = 512
UP_STEPS = TIN // UP_STEP


def first_kernel(
    index_ref,
    weight_ref,
    row_ref,
    grad_ref,
    hidden_ref,
    down_ref,
    up_ref,
    out_ref,
    pooled_out_ref,
    hid_ref,
    pooled_ref,
    group_ref,
    total_ref,
    sem,
):
    k = pl.program_id(0)

    @pl.when(k == 0)
    def _():
        for x in range(NX):
            left = jnp.concatenate([grad_ref[x, 0], grad_ref[x, 1]], axis=1)
            backward = lax.dot_general(left, down_ref[...], NT, preferred_element_type=F32)
            keep = hidden_ref[x * SAMP : (x + 1) * SAMP, :].astype(F32) > 0
            hid_ref[x * SAMP : (x + 1) * SAMP, :] = jnp.where(keep, backward, 0.0).astype(BF)

    result = lax.dot_general(hid_ref[...], up_ref[...], NT, preferred_element_type=F32)
    result = result.astype(BF).astype(F32)
    for x in range(NX):
        for j in range(UP_STEP // E):
            start = pl.multiple_of(x * FEAT * SAMP + (k * (UP_STEP // E) + j) * SAMP, SAMP)
            pooled_ref[pl.ds(start, SAMP), :] = result[
                x * SAMP : (x + 1) * SAMP, j * E : (j + 1) * E
            ]

    @pl.when(k == UP_STEPS - 1)
    def _():
        copy = pltpu.make_async_copy(pooled_ref, pooled_out_ref, sem)
        copy.start()
        add_elements(
            0, index_ref, weight_ref, row_ref, pooled_ref, group_ref, total_ref, out_ref
        )
        copy.wait()


def first_half(index, weight, rows, grads, hidden, down, up):
    whole = lambda shape: pl.BlockSpec(shape, lambda k: (0,) * len(shape))
    smem = pl.BlockSpec(memory_space=pltpu.SMEM)
    return pl.pallas_call(
        first_kernel,
        grid=(UP_STEPS,),
        out_shape=(
            jax.ShapeDtypeStruct((NZ, HALF, E), BF),
            jax.ShapeDtypeStruct((NX * FEAT * SAMP, E), F32),
        ),
        in_specs=[
            smem,
            smem,
            whole(rows.shape),
            whole(grads.shape),
            whole(hidden.shape),
            whole(down.shape),
            pl.BlockSpec((UP_STEP, HID), lambda k: (k, 0)),
        ],
        out_specs=(whole((NZ, HALF, E)), pl.BlockSpec(memory_space=pl.ANY)),
        scratch_shapes=[
            pltpu.VMEM((NX * SAMP, HID), BF),
            pltpu.VMEM((NX * FEAT * SAMP, E), F32),
            pltpu.VMEM((NX * LANES, E), F32),
            pltpu.VMEM((HALF, E), F32),
            pltpu.SemaphoreType.DMA,
        ],
        compiler_params=pltpu.CompilerParams(vmem_limit_bytes=40 << 20),
        cost_estimate=pl.CostEstimate(flops=5 << 30, bytes_accessed=20 << 20, transcendentals=0),
    )(index, weight, rows, grads, hidden, down, up)


def second_kernel(index_ref, weight_ref, row_ref, pooled_ref, out_ref, group_ref, total_ref):
    add_elements(1, index_ref, weight_ref, row_ref, pooled_ref, group_ref, total_ref, out_ref)


def second_half(index, weight, rows, pooled):
    smem = pl.BlockSpec(memory_space=pltpu.SMEM)
    vmem = pl.BlockSpec(memory_space=pltpu.VMEM)
    return pl.pallas_call(
        second_kernel,
        out_shape=jax.ShapeDtypeStruct((NZ, HALF, E), BF),
        in_specs=[smem, smem, vmem, vmem],
        out_specs=vmem,
        scratch_shapes=[pltpu.VMEM((NX * LANES, E), F32), pltpu.VMEM((HALF, E), F32)],
        compiler_params=pltpu.CompilerParams(vmem_limit_bytes=32 << 20),
        cost_estimate=pl.CostEstimate(flops=5 << 30, bytes_accessed=10 << 20, transcendentals=0),
    )(index, weight, rows, pooled)


def local(
    out_grad,
    hidden_pre,
    down_proj,
    up_proj,
    feature_slot,
    element_segment,
    element_weight,
    row_owner,
    row_local,
):
    hidden = lax.all_gather(hidden_pre[0], "x", tiled=True)
    arrived = lax.all_to_all(out_grad, "tower", split_axis=1, concat_axis=0, tiled=True)
    grad_rows = arrived.reshape(SAMP, TOUT)
    flat = (1, ELEMS)
    meta = bucket_elements(
        element_segment.reshape(flat),
        element_weight.reshape(flat),
        row_owner.reshape(flat),
        row_local.reshape(flat),
        feature_slot.reshape(FEAT, 1).astype(F32),
    )
    halves = jnp.stack([grad_rows[:, :LANES], grad_rows[:, LANES:]]).reshape(1, 2 * SAMP, LANES)
    outgoing = jnp.concatenate(
        [
            jnp.broadcast_to(halves, (NX, 2 * SAMP, LANES)),
            meta.reshape(NX, PIECES * CHUNKS * BUCKETS, LANES),
        ],
        axis=1,
    )
    incoming = lax.all_to_all(outgoing, "x", split_axis=0, concat_axis=0, tiled=True)
    grads = incoming[:, : 2 * SAMP].reshape(NX, 2, SAMP, LANES)
    parts = incoming[:, 2 * SAMP :].reshape(NX, PIECES, CHUNKS * BUCKETS, LANES).astype(F32)
    table = (NX * CHUNKS * BUCKETS, LANES)
    index = (parts[:, 0] * SAMP + parts[:, 1]).astype(I32).reshape(table)
    rows = parts[:, 2].astype(I32).reshape(table)
    weight = (parts[:, 3] + parts[:, 4] + parts[:, 5]).reshape(table)
    sums, pooled = first_half(index, weight, rows, grads, hidden, down_proj[0], up_proj[0])
    swap = functools.partial(
        lax.all_to_all, axis_name="z", split_axis=0, concat_axis=0, tiled=True
    )
    first = swap(sums)
    second = swap(second_half(index, weight, rows, pooled))
    table_grad = jnp.concatenate(
        [jnp.sum(first.astype(F32), axis=0), jnp.sum(second.astype(F32), axis=0)], axis=0
    )
    return table_grad.reshape(1, ROW_DEV, E)


def solution(mesh):
    towers = mesh.shape["tower"]
    grid = Mesh(mesh.devices.reshape(towers, NZ, NX), ("tower", "z", "x"))
    shard = ("z", "x")
    in_specs = (
        P(("tower", "z", "x"), None, None),
        P("tower", shard, None),
        P("tower", None, None),
        P("tower", None, None),
        P("tower", None),
        P("tower", shard, None),
        P("tower", shard, None),
        P("tower", shard, None, None),
        P("tower", shard, None),
    )
    out_specs = P("tower", shard, None)
    return jax.shard_map(local, mesh=grid, in_specs=in_specs, out_specs=out_specs, check_vma=False)
```

```python
import functools

import jax
import jax.numpy as jnp
from jax import lax
from jax.experimental import pallas as pl
from jax.experimental.pallas import tpu as pltpu
from jax.sharding import Mesh
from jax.sharding import PartitionSpec as P

E = 128
FEAT = 32
SAMP = 128
HID = 1024
TOUT = 256
TIN = 4096
ROW_DEV = 512
ELEMS = 5120
CAP = 320
NX = 4
NZ = 8
HALVES = 2
HALF = ROW_DEV // HALVES
BUCKETS = NZ * HALVES
SUBS = NX * BUCKETS
PIECES = 5
SLOTS = 384
LANES = 128
CHUNKS = SLOTS // LANES
STEP = 512
UNROLL = 16
BF = jnp.bfloat16
F32 = jnp.float32
I32 = jnp.int32
NT = (((1,), (1,)), ((), ()))


def bucket_kernel(seg_ref, weight_ref, owner_ref, row_ref, slot_ref, out_ref, acc_ref):
    upper = (
        lax.broadcasted_iota(I32, (STEP, STEP), 0) <= lax.broadcasted_iota(I32, (STEP, STEP), 1)
    ).astype(F32).astype(BF)
    sub_ids = lax.broadcasted_iota(I32, (SUBS, STEP), 0)
    feat_ids = lax.broadcasted_iota(I32, (FEAT, STEP), 0)
    slot_ids = lax.broadcasted_iota(I32, (SLOTS, STEP), 0).astype(F32)
    acc_ref[...] = jnp.zeros_like(acc_ref)

    def step(k, carry):
        cols = pl.ds(pl.multiple_of(k * STEP, STEP), STEP)
        seg = seg_ref[:, cols]
        weight = weight_ref[:, cols]
        owner = owner_ref[:, cols]
        row = row_ref[:, cols]
        sub = (owner & 3) * BUCKETS + (row >> 8) * NZ + (owner >> 2)
        mine = sub_ids == sub
        ones = jnp.where(mine, 1.0, 0.0)
        inclusive = jnp.dot(ones.astype(BF), upper, preferred_element_type=F32) + carry
        rank = jnp.sum(ones * inclusive, axis=0, keepdims=True) - 1.0
        block = jnp.sum(
            jnp.where(feat_ids == (seg & 31), slot_ref[...], 0.0), axis=0, keepdims=True
        )
        sample = (seg >> 5).astype(F32)
        row_next = ((row & 255) + 1).astype(F32)
        high = weight.astype(BF).astype(F32)
        rest = weight - high
        middle = rest.astype(BF).astype(F32)
        pieces = (block, sample, row_next, high, middle)
        left = jnp.concatenate([(ones * piece).astype(BF) for piece in pieces], axis=0)
        right = jnp.where(slot_ids == rank, 1.0, 0.0).astype(BF)
        acc_ref[...] += lax.dot_general(left, right, NT, preferred_element_type=F32)
        return inclusive[:, STEP - 1 : STEP]

    count = lax.fori_loop(0, ELEMS // STEP, step, jnp.zeros((SUBS, 1), F32))
    count = jnp.broadcast_to(count.astype(I32), (SUBS, LANES))
    count_parts = ((count >> 7).astype(F32), (count & 127).astype(F32))
    spare = lax.broadcasted_iota(I32, (SUBS, LANES), 1) >= CAP - (CHUNKS - 1) * LANES
    for p in range(PIECES):
        for c in range(CHUNKS):
            part = acc_ref[p * SUBS : (p + 1) * SUBS, c * LANES : (c + 1) * LANES]
            if p < 2 and c == CHUNKS - 1:
                part = jnp.where(spare, count_parts[p], part)
            part = part.astype(BF)
            for x in range(NX):
                out_ref[x, p, c] = part[x * BUCKETS : (x + 1) * BUCKETS]


def bucket_elements(segment, weight, owner, row, slots):
    return pl.pallas_call(
        bucket_kernel,
        out_shape=jax.ShapeDtypeStruct((NX, PIECES, CHUNKS, BUCKETS, LANES), BF),
        in_specs=[pl.BlockSpec(memory_space=pltpu.VMEM)] * 5,
        out_specs=pl.BlockSpec(memory_space=pltpu.VMEM),
        scratch_shapes=[pltpu.VMEM((PIECES * SUBS, SLOTS), F32)],
        compiler_params=pltpu.CompilerParams(vmem_limit_bytes=32 << 20),
        cost_estimate=pl.CostEstimate(flops=3 << 30, bytes_accessed=1 << 20, transcendentals=0),
    )(segment, weight, owner, row, slots)


def add_elements(
    half, index_ref, weight_ref, row_ref, pooled_ref, group_ref, spill_ref, total_ref, out_ref
):
    group_ref[...] = jnp.zeros_like(group_ref)
    spill_ref[...] = jnp.zeros_like(spill_ref)

    def place_of(i):
        return (i & (NX - 1)) * (CHUNKS * BUCKETS) + half * NZ + (i >> 2)

    def count_of(place):
        return index_ref[
            (place + (CHUNKS - 1) * BUCKETS) * LANES + CAP - (CHUNKS - 1) * LANES
        ]

    def fetch(place, count, target_ref, start):
        def some(j, unused):
            source = place * LANES + j * UNROLL
            target = pl.multiple_of(start + j * UNROLL, UNROLL)
            for u in range(UNROLL):
                value = pooled_ref[pl.ds(index_ref[source + u], 1), :] * weight_ref[source + u]
                target_ref[pl.ds(target + u, 1), :] = value
            return unused

        lax.fori_loop(0, (count + (UNROLL - 1)) // UNROLL, some, 0)

    def bucket_step(i, unused):
        place = place_of(i)
        fetch(place, jnp.minimum(count_of(place), LANES), group_ref, i * LANES)
        return unused

    lax.fori_loop(0, NZ * NX, bucket_step, 0)

    def chosen(rows):
        row_ids = lax.broadcasted_iota(I32, (HALF, rows.shape[1]), 0) + 1
        return jnp.where(row_ids == rows, 1.0, 0.0).astype(BF)

    for o in range(NZ):
        rows = jnp.concatenate(
            [
                row_ref[pl.ds(x * CHUNKS * BUCKETS + half * NZ + o, 1), :]
                for x in range(NX)
            ],
            axis=1,
        )
        values = group_ref[o * NX * LANES : (o + 1) * NX * LANES, :].astype(BF)
        total_ref[o] = jnp.dot(chosen(rows), values, preferred_element_type=F32)

    def spill_step(i, unused):
        place = place_of(i)
        count = count_of(place)

        def chunk_step(c, unused):
            there = place + c * BUCKETS
            fetch(there, jnp.minimum(count - c * LANES, LANES), spill_ref, 0)
            total_ref[i >> 2] += jnp.dot(
                chosen(row_ref[pl.ds(there, 1), :]),
                spill_ref[...].astype(BF),
                preferred_element_type=F32,
            )
            return unused

        return lax.fori_loop(1, (count + (LANES - 1)) // LANES, chunk_step, unused)

    lax.fori_loop(0, NZ * NX, spill_step, 0)
    out_ref[...] = total_ref[...].astype(BF)


SCRATCH = (
    pltpu.VMEM((NZ * NX * LANES, E), F32),
    pltpu.VMEM((LANES, E), F32),
    pltpu.VMEM((NZ, HALF, E), F32),
)
UP_STEP = 512
UP_STEPS = TIN // UP_STEP


def first_kernel(
    me_ref,
    index_ref,
    weight_ref,
    row_ref,
    grad_ref,
    hidden0_ref,
    hidden1_ref,
    hidden2_ref,
    hidden3_ref,
    down_ref,
    up_ref,
    out_ref,
    pooled_out_ref,
    hid_ref,
    pooled_ref,
    group_ref,
    spill_ref,
    total_ref,
    sem,
):
    k = pl.program_id(0)

    @pl.when(k == 0)
    def _():
        for r, hidden_ref in enumerate((hidden0_ref, hidden1_ref, hidden2_ref, hidden3_ref)):
            x = (me_ref[0] + (NX - r)) & (NX - 1)
            left = jnp.concatenate([grad_ref[x, 0], grad_ref[x, 1]], axis=1)
            backward = lax.dot_general(left, down_ref[...], NT, preferred_element_type=F32)
            keep = hidden_ref[...].astype(F32) > 0
            there = pl.ds(pl.multiple_of(x * SAMP, SAMP), SAMP)
            hid_ref[there, :] = jnp.where(keep, backward, 0.0).astype(BF)

    result = lax.dot_general(hid_ref[...], up_ref[...], NT, preferred_element_type=F32)
    result = result.astype(BF).astype(F32)
    for x in range(NX):
        for j in range(UP_STEP // E):
            start = pl.multiple_of(x * FEAT * SAMP + (k * (UP_STEP // E) + j) * SAMP, SAMP)
            pooled_ref[pl.ds(start, SAMP), :] = result[
                x * SAMP : (x + 1) * SAMP, j * E : (j + 1) * E
            ]

    @pl.when(k == UP_STEPS - 1)
    def _():
        copy = pltpu.make_async_copy(pooled_ref, pooled_out_ref, sem)
        copy.start()
        add_elements(
            0,
            index_ref,
            weight_ref,
            row_ref,
            pooled_ref,
            group_ref,
            spill_ref,
            total_ref,
            out_ref,
        )
        copy.wait()


def first_half(me, index, weight, rows, grads, hiddens, down, up):
    whole = lambda shape: pl.BlockSpec(shape, lambda k: (0,) * len(shape))
    smem = pl.BlockSpec(memory_space=pltpu.SMEM)
    return pl.pallas_call(
        first_kernel,
        grid=(UP_STEPS,),
        out_shape=(
            jax.ShapeDtypeStruct((NZ, HALF, E), BF),
            pltpu.HBM((NX * FEAT * SAMP, E), F32),
        ),
        in_specs=[
            smem,
            smem,
            smem,
            whole(rows.shape),
            whole(grads.shape),
            *[whole((SAMP, HID))] * NX,
            whole(down.shape),
            pl.BlockSpec((UP_STEP, HID), lambda k: (k, 0)),
        ],
        out_specs=(whole((NZ, HALF, E)), pl.BlockSpec(memory_space=pltpu.HBM)),
        scratch_shapes=[
            pltpu.VMEM((NX * SAMP, HID), BF),
            pltpu.VMEM((NX * FEAT * SAMP, E), F32),
            *SCRATCH,
            pltpu.SemaphoreType.DMA,
        ],
        compiler_params=pltpu.CompilerParams(vmem_limit_bytes=40 << 20),
        cost_estimate=pl.CostEstimate(flops=5 << 30, bytes_accessed=20 << 20, transcendentals=0),
    )(me, index, weight, rows, grads, *hiddens, down, up)


def second_kernel(
    index_ref, weight_ref, row_ref, pooled_hbm_ref, out_ref, pooled_ref, group_ref, spill_ref,
    total_ref, sem,
):
    copy = pltpu.make_async_copy(pooled_hbm_ref, pooled_ref, sem)
    copy.start()
    copy.wait()
    add_elements(
        1, index_ref, weight_ref, row_ref, pooled_ref, group_ref, spill_ref, total_ref, out_ref
    )


def second_half(index, weight, rows, pooled):
    smem = pl.BlockSpec(memory_space=pltpu.SMEM)
    vmem = pl.BlockSpec(memory_space=pltpu.VMEM)
    return pl.pallas_call(
        second_kernel,
        out_shape=jax.ShapeDtypeStruct((NZ, HALF, E), BF),
        in_specs=[smem, smem, vmem, pl.BlockSpec(memory_space=pltpu.HBM)],
        out_specs=vmem,
        scratch_shapes=[
            pltpu.VMEM((NX * FEAT * SAMP, E), F32),
            *SCRATCH,
            pltpu.SemaphoreType.DMA,
        ],
        compiler_params=pltpu.CompilerParams(vmem_limit_bytes=32 << 20),
        cost_estimate=pl.CostEstimate(flops=5 << 30, bytes_accessed=10 << 20, transcendentals=0),
    )(index, weight, rows, pltpu.with_memory_space_constraint(pooled, pltpu.HBM))


def local(
    out_grad,
    hidden_pre,
    down_proj,
    up_proj,
    feature_slot,
    element_segment,
    element_weight,
    row_owner,
    row_local,
):
    hidden = hidden_pre[0]
    hiddens = [hidden] + [
        lax.ppermute(hidden, "x", [(i, (i + shift) % NX) for i in range(NX)])
        for shift in range(1, NX)
    ]
    arrived = lax.all_to_all(out_grad, "tower", split_axis=1, concat_axis=0, tiled=True)
    grad_rows = arrived.reshape(SAMP, TOUT)
    flat = (1, ELEMS)
    meta = bucket_elements(
        element_segment.reshape(flat),
        element_weight.reshape(flat),
        row_owner.reshape(flat),
        row_local.reshape(flat),
        feature_slot.reshape(FEAT, 1).astype(F32),
    )
    halves = jnp.stack([grad_rows[:, :LANES], grad_rows[:, LANES:]]).reshape(1, 2 * SAMP, LANES)
    outgoing = jnp.concatenate(
        [
            jnp.broadcast_to(halves, (NX, 2 * SAMP, LANES)),
            meta.reshape(NX, PIECES * CHUNKS * BUCKETS, LANES),
        ],
        axis=1,
    )
    incoming = lax.all_to_all(outgoing, "x", split_axis=0, concat_axis=0, tiled=True)
    grads = incoming[:, : 2 * SAMP].reshape(NX, 2, SAMP, LANES)
    parts = incoming[:, 2 * SAMP :].reshape(NX, PIECES, CHUNKS * BUCKETS, LANES).astype(F32)
    shape = (NX, CHUNKS * BUCKETS, LANES)
    slot = lax.broadcasted_iota(I32, shape, 1) // BUCKETS * LANES + lax.broadcasted_iota(
        I32, shape, 2
    )
    offset = jnp.where(slot < CAP, lax.broadcasted_iota(I32, shape, 0) * (FEAT * SAMP), 0)
    index = ((parts[:, 0] * SAMP + parts[:, 1]).astype(I32) + offset).reshape(-1)
    rows = parts[:, 2].astype(I32).reshape(NX * CHUNKS * BUCKETS, LANES)
    weight = (parts[:, 3] + parts[:, 4]).reshape(-1)
    me = lax.axis_index("x").astype(I32).reshape(1)
    sums, pooled = first_half(
        me, index, weight, rows, grads, hiddens, down_proj[0], up_proj[0]
    )
    swap = functools.partial(
        lax.all_to_all, axis_name="z", split_axis=0, concat_axis=0, tiled=True
    )
    first = swap(sums)
    second = swap(second_half(index, weight, rows, pooled))
    table_grad = jnp.concatenate(
        [jnp.sum(first.astype(F32), axis=0), jnp.sum(second.astype(F32), axis=0)], axis=0
    )
    return table_grad.reshape(1, ROW_DEV, E)


def solution(mesh):
    towers = mesh.shape["tower"]
    grid = Mesh(mesh.devices.reshape(towers, NZ, NX), ("tower", "z", "x"))
    shard = ("z", "x")
    in_specs = (
        P(("tower", "z", "x"), None, None),
        P("tower", shard, None),
        P("tower", None, None),
        P("tower", None, None),
        P("tower", None),
        P("tower", shard, None),
        P("tower", shard, None),
        P("tower", shard, None, None),
        P("tower", shard, None),
    )
    out_specs = P("tower", shard, None)
    return jax.shard_map(local, mesh=grid, in_specs=in_specs, out_specs=out_specs, check_vma=False)
```

```python
import functools

import jax
import jax.numpy as jnp
from jax import lax
from jax.experimental import pallas as pl
from jax.experimental.pallas import tpu as pltpu
from jax.sharding import Mesh
from jax.sharding import PartitionSpec as P

E = 128
FEAT = 32
SAMP = 128
HID = 1024
TOUT = 256
TIN = 4096
ROW_DEV = 512
ELEMS = 5120
CAP = 320
NX = 4
NZ = 8
HALVES = 2
HALF = ROW_DEV // HALVES
BUCKETS = NZ * HALVES
SUBS = NX * BUCKETS
PIECES = 5
SLOTS = 384
LANES = 128
CHUNKS = SLOTS // LANES
USED = 120
STEP = 512
UNROLL = 16
BF = jnp.bfloat16
F32 = jnp.float32
I32 = jnp.int32
NT = (((1,), (1,)), ((), ()))


def in_hbm(operand):
    return pltpu.with_memory_space_constraint(operand, pltpu.HBM)


def in_vmem(operand):
    return pltpu.with_memory_space_constraint(operand, pltpu.VMEM)


def bucket_kernel(
    seg_ref,
    weight_ref,
    owner_ref,
    row_ref,
    slot_ref,
    up_hbm_ref,
    after_ref,
    out_ref,
    up_ref,
    acc_ref,
    up_sem,
):
    del after_ref
    up_copy = pltpu.make_async_copy(up_hbm_ref, up_ref, up_sem)
    up_copy.start()
    square = (FEAT, FEAT)
    diagonal = lax.broadcasted_iota(I32, square, 0) == lax.broadcasted_iota(I32, square, 1)
    slots = jnp.sum(
        jnp.where(diagonal, slot_ref[...].astype(F32), 0.0), axis=1, keepdims=True
    )
    upper = (
        lax.broadcasted_iota(I32, (STEP, STEP), 0) <= lax.broadcasted_iota(I32, (STEP, STEP), 1)
    ).astype(F32).astype(BF)
    sub_ids = lax.broadcasted_iota(I32, (SUBS, STEP), 0)
    feat_ids = lax.broadcasted_iota(I32, (FEAT, STEP), 0)
    slot_ids = lax.broadcasted_iota(I32, (SLOTS, STEP), 0).astype(F32)
    acc_ref[...] = jnp.zeros_like(acc_ref)

    def step(k, carry):
        cols = pl.ds(pl.multiple_of(k * STEP, STEP), STEP)
        seg = seg_ref[:, cols]
        weight = weight_ref[:, cols]
        owner = owner_ref[:, cols]
        row = row_ref[:, cols]
        sub = (owner & 3) * BUCKETS + (row >> 8) * NZ + (owner >> 2)
        mine = sub_ids == sub
        ones = jnp.where(mine, 1.0, 0.0)
        inclusive = jnp.dot(ones.astype(BF), upper, preferred_element_type=F32) + carry
        rank = jnp.sum(ones * inclusive, axis=0, keepdims=True) - 1.0
        block = jnp.sum(
            jnp.where(feat_ids == (seg & 31), slots, 0.0), axis=0, keepdims=True
        )
        sample = (seg >> 5).astype(F32)
        row_next = ((row & 255) + 1).astype(F32)
        high = weight.astype(BF).astype(F32)
        rest = weight - high
        middle = rest.astype(BF).astype(F32)
        pieces = (block, sample, row_next, high, middle)
        left = jnp.concatenate([(ones * piece).astype(BF) for piece in pieces], axis=0)
        place = rank
        for c in range(1, CHUNKS):
            place = place + jnp.where(rank >= c * USED, float(LANES - USED), 0.0)
        right = jnp.where(slot_ids == place, 1.0, 0.0).astype(BF)
        acc_ref[...] += lax.dot_general(left, right, NT, preferred_element_type=F32)
        return inclusive[:, STEP - 1 : STEP]

    count = lax.fori_loop(0, ELEMS // STEP, step, jnp.zeros((SUBS, 1), F32), unroll=10)
    count = jnp.broadcast_to(count.astype(I32), (SUBS, LANES))
    count_parts = ((count >> 7).astype(F32), (count & 127).astype(F32))
    spare = lax.broadcasted_iota(I32, (SUBS, LANES), 1) >= USED
    for p in range(PIECES):
        for c in range(CHUNKS):
            part = acc_ref[p * SUBS : (p + 1) * SUBS, c * LANES : (c + 1) * LANES]
            if p < 2 and c == 0:
                part = jnp.where(spare, count_parts[p], part)
            part = part.astype(BF)
            for x in range(NX):
                out_ref[x, p, c] = part[x * BUCKETS : (x + 1) * BUCKETS]
    up_copy.wait()


def bucket_elements(segment, weight, owner, row, slots, up, after):
    vmem = pl.BlockSpec(memory_space=pltpu.VMEM)
    operands = (segment, weight, owner, row, slots, up)
    return pl.pallas_call(
        bucket_kernel,
        out_shape=(
            jax.ShapeDtypeStruct((NX, PIECES, CHUNKS, BUCKETS, LANES), BF),
            pltpu.VMEM((TIN, HID), BF),
        ),
        in_specs=[vmem] * 5
        + [pl.BlockSpec(memory_space=pltpu.HBM), pl.BlockSpec(memory_space=pl.ANY)],
        out_specs=(vmem, vmem),
        scratch_shapes=[pltpu.VMEM((PIECES * SUBS, SLOTS), F32), pltpu.SemaphoreType.DMA],
        compiler_params=pltpu.CompilerParams(vmem_limit_bytes=24 << 20),
        cost_estimate=pl.CostEstimate(flops=3 << 30, bytes_accessed=9 << 20, transcendentals=0),
    )(*[in_hbm(operand) for operand in operands], after)


def chosen(rows):
    row_ids = lax.broadcasted_iota(I32, (HALF, rows.shape[1]), 0) + 1
    return jnp.where(row_ids == rows, 1.0, 0.0).astype(BF)


def table_kernel(
    half,
    index_hbm_ref,
    weight_ref,
    row_ref,
    pooled_ref,
    out_ref,
    group_ref,
    spill_ref,
    total_ref,
    index_ref,
    index_sems,
):
    part = NZ * LANES

    def index_copy(c, x):
        start = ((x * CHUNKS + c) * BUCKETS + half * NZ) * LANES
        return pltpu.make_async_copy(
            index_hbm_ref.at[pl.ds(start, part)],
            index_ref.at[pl.ds((c * NX + x) * part, part)],
            index_sems.at[c, x],
        )

    for c in range(CHUNKS):
        for x in range(NX):
            index_copy(c, x).start()
    group_ref[...] = jnp.zeros_like(group_ref)
    spill_ref[...] = jnp.zeros_like(spill_ref)

    def vector_row(c, x, o):
        return pl.ds((x * CHUNKS + c) * BUCKETS + half * NZ + o, 1)

    def index_row(c, x, o):
        return ((c * NX + x) * NZ + o) * LANES

    def fetch(source_row, count, shift, target_ref, start):
        def some(j, unused):
            source = source_row + j * UNROLL
            target = pl.multiple_of(start + j * UNROLL, UNROLL)
            for u in range(UNROLL):
                target_ref[pl.ds(target + u, 1), :] = pooled_ref[
                    pl.ds(index_ref[source + u] + shift, 1), :
                ]
            return unused

        lax.fori_loop(0, (count + (UNROLL - 1)) // UNROLL, some, 0)

    for x in range(NX):
        index_copy(0, x).wait()

        def bucket_step(o, unused, x=x):
            row = index_row(0, x, o)
            count = jnp.minimum(index_ref[row + USED], USED)
            fetch(row, count, x * (FEAT * SAMP), group_ref, (o * NX + x) * LANES)
            return unused

        lax.fori_loop(0, NZ, bucket_step, 0)
    blank = jnp.zeros((8 - NX, LANES), F32)
    for o in range(NZ):
        rows = jnp.concatenate([row_ref[vector_row(0, x, o), :] for x in range(NX)], axis=1)
        weights = [weight_ref[vector_row(0, x, o), :] for x in range(NX)]
        columns = jnp.concatenate([*weights, blank], axis=0).T
        values = []
        for x in range(NX):
            start = (o * NX + x) * LANES
            values.append(group_ref[start : start + LANES, :] * columns[:, x : x + 1])
        values = jnp.concatenate(values, axis=0).astype(BF)
        total_ref[o] = jnp.dot(chosen(rows), values, preferred_element_type=F32)
    for c in range(1, CHUNKS):
        for x in range(NX):
            index_copy(c, x).wait()

    def spill_step(i, unused):
        x, o = i & (NX - 1), i >> 2
        count = index_ref[index_row(0, x, o) + USED]

        def chunk_step(c, unused):
            rest = jnp.minimum(count - c * USED, USED)
            fetch(index_row(c, x, o), rest, x * (FEAT * SAMP), spill_ref, 0)
            weight = weight_ref[vector_row(c, x, o), :]
            column = jnp.broadcast_to(weight, (8, LANES)).T[:, :1]
            total_ref[o] += jnp.dot(
                chosen(row_ref[vector_row(c, x, o), :]),
                (spill_ref[...] * column).astype(BF),
                preferred_element_type=F32,
            )
            return unused

        return lax.fori_loop(1, (count + (USED - 1)) // USED, chunk_step, unused)

    lax.fori_loop(0, NX * NZ, spill_step, 0)
    out_ref[...] = total_ref[...].astype(BF)


def half_tables(half, index, weight, rows, pooled):
    hbm = pl.BlockSpec(memory_space=pltpu.HBM)
    vmem = pl.BlockSpec(memory_space=pltpu.VMEM)
    return pl.pallas_call(
        functools.partial(table_kernel, half),
        out_shape=jax.ShapeDtypeStruct((NZ, HALF, E), BF),
        in_specs=[hbm, vmem, vmem, vmem],
        out_specs=vmem,
        scratch_shapes=[
            pltpu.VMEM((NZ * NX * LANES, E), F32),
            pltpu.VMEM((LANES, E), F32),
            pltpu.VMEM((NZ, HALF, E), F32),
            pltpu.SMEM((CHUNKS * NX * NZ * LANES,), I32),
            pltpu.SemaphoreType.DMA((CHUNKS, NX)),
        ],
        compiler_params=pltpu.CompilerParams(vmem_limit_bytes=24 << 20),
        cost_estimate=pl.CostEstimate(flops=5 << 30, bytes_accessed=10 << 20, transcendentals=0),
    )(in_hbm(index), weight, rows, in_vmem(pooled))


UP_STEP = 1024
UP_STEPS = TIN // UP_STEP
UP_PART = 512


def pooled_kernel(
    me_ref,
    grad_ref,
    hidden0_ref,
    hidden1_ref,
    hidden2_ref,
    hidden3_ref,
    down_ref,
    up_ref,
    pooled_ref,
    hid_ref,
):
    for r, hidden_ref in enumerate((hidden0_ref, hidden1_ref, hidden2_ref, hidden3_ref)):
        x = (me_ref[0] + (NX - r)) & (NX - 1)
        backward = lax.dot_general(grad_ref[x], down_ref[...], NT, preferred_element_type=F32)
        keep = hidden_ref[...].astype(F32) > 0
        there = pl.ds(pl.multiple_of(x * SAMP, SAMP), SAMP)
        hid_ref[there, :] = jnp.where(keep, backward, 0.0).astype(BF)

    def up_step(k, unused):
        for j in range(UP_STEP // UP_PART):
            rows = pl.ds(pl.multiple_of(k * UP_STEP + j * UP_PART, UP_PART), UP_PART)
            result = lax.dot_general(
                hid_ref[...], up_ref[rows, :], NT, preferred_element_type=F32
            )
            result = result.astype(BF).astype(F32)
            for x in range(NX):
                for i in range(UP_PART // E):
                    block = (k * UP_STEP + j * UP_PART) // E + i
                    start = pl.multiple_of((x * FEAT + block) * SAMP, SAMP)
                    pooled_ref[pl.ds(start, SAMP), :] = result[
                        x * SAMP : (x + 1) * SAMP, i * E : (i + 1) * E
                    ]
        return unused

    lax.fori_loop(0, UP_STEPS, up_step, 0)


def pooled_gradients(me, grads, hiddens, down, up):
    vmem = pl.BlockSpec(memory_space=pltpu.VMEM)
    smem = pl.BlockSpec(memory_space=pltpu.SMEM)
    return pl.pallas_call(
        pooled_kernel,
        out_shape=pltpu.VMEM((NX * FEAT * SAMP, E), F32),
        in_specs=[smem, vmem, *[vmem] * NX, vmem, vmem],
        out_specs=vmem,
        scratch_shapes=[pltpu.VMEM((NX * SAMP, HID), BF)],
        compiler_params=pltpu.CompilerParams(vmem_limit_bytes=24 << 20),
        cost_estimate=pl.CostEstimate(flops=5 << 30, bytes_accessed=20 << 20, transcendentals=0),
    )(me, grads, *hiddens, down, in_vmem(up))


def local(
    out_grad,
    hidden_pre,
    down_proj,
    up_proj,
    feature_slot,
    element_segment,
    element_weight,
    row_owner,
    row_local,
):
    hidden = hidden_pre[0]
    hiddens = [hidden] + [
        lax.ppermute(hidden, "x", [(i, (i + shift) % NX) for i in range(NX)])
        for shift in range(1, NX)
    ]
    arrived = lax.all_to_all(out_grad, "tower", split_axis=1, concat_axis=0, tiled=True)
    swap_x = functools.partial(
        lax.all_to_all, axis_name="x", split_axis=0, concat_axis=0, tiled=True
    )
    grads = swap_x(jnp.broadcast_to(arrived.reshape(1, SAMP, TOUT), (NX, SAMP, TOUT)))
    flat = (1, ELEMS)
    buckets, up = bucket_elements(
        element_segment.reshape(flat),
        element_weight.reshape(flat),
        row_owner.reshape(flat),
        row_local.reshape(flat),
        feature_slot,
        up_proj[0],
        arrived,
    )
    buckets = swap_x(buckets)
    parts = buckets.reshape(NX, PIECES, CHUNKS * BUCKETS, LANES).astype(F32)
    index = (parts[:, 0] * SAMP + parts[:, 1]).astype(I32).reshape(-1)
    rows = parts[:, 2].astype(I32).reshape(NX * CHUNKS * BUCKETS, LANES)
    weight = (parts[:, 3] + parts[:, 4]).reshape(NX * CHUNKS * BUCKETS, LANES)
    me = lax.axis_index("x").astype(I32).reshape(1)
    pooled = pooled_gradients(me, grads, hiddens, down_proj[0], up)
    swap = functools.partial(
        lax.all_to_all, axis_name="z", split_axis=0, concat_axis=0, tiled=True
    )
    first = swap(half_tables(0, index, weight, rows, pooled))
    second = swap(half_tables(1, index, weight, rows, pooled))
    table_grad = jnp.concatenate(
        [jnp.sum(first.astype(F32), axis=0), jnp.sum(second.astype(F32), axis=0)], axis=0
    )
    return table_grad.reshape(1, ROW_DEV, E)


def solution(mesh):
    towers = mesh.shape["tower"]
    grid = Mesh(mesh.devices.reshape(towers, NZ, NX), ("tower", "z", "x"))
    shard = ("z", "x")
    in_specs = (
        P(("tower", "z", "x"), None, None),
        P("tower", shard, None),
        P("tower", None, None),
        P("tower", None, None),
        P("tower", None),
        P("tower", shard, None),
        P("tower", shard, None),
        P("tower", shard, None, None),
        P("tower", shard, None),
    )
    out_specs = P("tower", shard, None)
    return jax.shard_map(local, mesh=grid, in_specs=in_specs, out_specs=out_specs, check_vma=False)
```

```python
import functools

import jax
import jax.numpy as jnp
from jax import lax
from jax.experimental import pallas as pl
from jax.experimental.pallas import tpu as pltpu
from jax.sharding import Mesh
from jax.sharding import PartitionSpec as P

E = 128
FEAT = 32
SAMP = 128
HID = 1024
TOUT = 256
TIN = 4096
ROW_DEV = 512
ELEMS = 5120
CAP = 320
NX = 4
NZ = 8
HALVES = 2
HALF = ROW_DEV // HALVES
BUCKETS = NZ * HALVES
SUBS = NX * BUCKETS
PIECES = 5
SLOTS = 384
LANES = 128
CHUNKS = SLOTS // LANES
USED = 120
STEP = 512
UNROLL = 16
BF = jnp.bfloat16
F32 = jnp.float32
I32 = jnp.int32
NT = (((1,), (1,)), ((), ()))


def in_hbm(operand):
    return pltpu.with_memory_space_constraint(operand, pltpu.HBM)


def bucket_kernel(
    seg_ref,
    weight_ref,
    owner_ref,
    row_ref,
    slot_ref,
    after_ref,
    out_ref,
    acc_ref,
):
    del after_ref
    square = (FEAT, FEAT)
    diagonal = lax.broadcasted_iota(I32, square, 0) == lax.broadcasted_iota(I32, square, 1)
    slots = jnp.sum(
        jnp.where(diagonal, slot_ref[...].astype(F32), 0.0), axis=1, keepdims=True
    )
    upper = (
        lax.broadcasted_iota(I32, (STEP, STEP), 0) <= lax.broadcasted_iota(I32, (STEP, STEP), 1)
    ).astype(F32).astype(BF)
    sub_ids = lax.broadcasted_iota(I32, (SUBS, STEP), 0)
    feat_ids = lax.broadcasted_iota(I32, (FEAT, STEP), 0)
    slot_ids = lax.broadcasted_iota(I32, (SLOTS, STEP), 0).astype(F32)
    acc_ref[...] = jnp.zeros_like(acc_ref)

    def step(k, carry):
        cols = pl.ds(pl.multiple_of(k * STEP, STEP), STEP)
        seg = seg_ref[:, cols]
        weight = weight_ref[:, cols]
        owner = owner_ref[:, cols]
        row = row_ref[:, cols]
        sub = (owner & 3) * BUCKETS + (row >> 8) * NZ + (owner >> 2)
        mine = sub_ids == sub
        ones = jnp.where(mine, 1.0, 0.0)
        inclusive = jnp.dot(ones.astype(BF), upper, preferred_element_type=F32) + carry
        rank = jnp.sum(ones * inclusive, axis=0, keepdims=True) - 1.0
        block = jnp.sum(
            jnp.where(feat_ids == (seg & 31), slots, 0.0), axis=0, keepdims=True
        )
        sample = (seg >> 5).astype(F32)
        row_next = ((row & 255) + 1).astype(F32)
        high = weight.astype(BF).astype(F32)
        rest = weight - high
        middle = rest.astype(BF).astype(F32)
        pieces = (block, sample, row_next, high, middle)
        left = jnp.concatenate([(ones * piece).astype(BF) for piece in pieces], axis=0)
        place = rank
        for c in range(1, CHUNKS):
            place = place + jnp.where(rank >= c * USED, float(LANES - USED), 0.0)
        right = jnp.where(slot_ids == place, 1.0, 0.0).astype(BF)
        acc_ref[...] += lax.dot_general(left, right, NT, preferred_element_type=F32)
        return inclusive[:, STEP - 1 : STEP]

    count = lax.fori_loop(0, ELEMS // STEP, step, jnp.zeros((SUBS, 1), F32), unroll=10)
    count = jnp.broadcast_to(count.astype(I32), (SUBS, LANES))
    count_parts = ((count >> 7).astype(F32), (count & 127).astype(F32))
    spare = lax.broadcasted_iota(I32, (SUBS, LANES), 1) >= USED
    for p in range(PIECES):
        for c in range(CHUNKS):
            part = acc_ref[p * SUBS : (p + 1) * SUBS, c * LANES : (c + 1) * LANES]
            if p < 2 and c == 0:
                part = jnp.where(spare, count_parts[p], part)
            part = part.astype(BF)
            for x in range(NX):
                out_ref[x, p, c] = part[x * BUCKETS : (x + 1) * BUCKETS]


def bucket_elements(segment, weight, owner, row, slots, after):
    vmem = pl.BlockSpec(memory_space=pltpu.VMEM)
    operands = (segment, weight, owner, row, slots)
    return pl.pallas_call(
        bucket_kernel,
        out_shape=jax.ShapeDtypeStruct((NX, PIECES, CHUNKS, BUCKETS, LANES), BF),
        in_specs=[vmem] * 5 + [pl.BlockSpec(memory_space=pl.ANY)],
        out_specs=vmem,
        scratch_shapes=[pltpu.VMEM((PIECES * SUBS, SLOTS), F32)],
        compiler_params=pltpu.CompilerParams(vmem_limit_bytes=24 << 20),
        cost_estimate=pl.CostEstimate(flops=3 << 30, bytes_accessed=1 << 20, transcendentals=0),
    )(*[in_hbm(operand) for operand in operands], after)


def chosen(rows):
    row_ids = lax.broadcasted_iota(I32, (HALF, rows.shape[1]), 0) + 1
    return jnp.where(row_ids == rows, 1.0, 0.0).astype(BF)


TABLE_SCRATCH = (
    pltpu.VMEM((NZ * NX * LANES, E), F32),
    pltpu.VMEM((LANES, E), F32),
    pltpu.VMEM((NZ, HALF, E), F32),
    pltpu.SMEM((CHUNKS * NX * NZ * LANES,), I32),
    pltpu.SMEM((NX * NZ + 1,), I32),
    pltpu.SemaphoreType.DMA((CHUNKS, NX)),
)


class Table:
    def __init__(
        self, half, index_hbm_ref, weight_ref, row_ref, pooled_ref, out_ref, scratch
    ):
        self.half = half
        self.pooled_ref = pooled_ref
        self.index_hbm_ref, self.weight_ref, self.row_ref = index_hbm_ref, weight_ref, row_ref
        self.out_ref = out_ref
        self.group_ref, self.spill_ref, self.total_ref = scratch[:3]
        self.index_ref, self.spilled_ref, self.index_sems = scratch[3:]

    def index_copy(self, c, x):
        part = NZ * LANES
        start = ((x * CHUNKS + c) * BUCKETS + self.half * NZ) * LANES
        return pltpu.make_async_copy(
            self.index_hbm_ref.at[pl.ds(start, part)],
            self.index_ref.at[pl.ds((c * NX + x) * part, part)],
            self.index_sems.at[c, x],
        )

    def begin(self):
        for c in range(CHUNKS):
            for x in range(NX):
                self.index_copy(c, x).start()
        self.group_ref[...] = jnp.zeros_like(self.group_ref)
        self.spill_ref[...] = jnp.zeros_like(self.spill_ref)

    def vector_row(self, c, x, o):
        return pl.ds((x * CHUNKS + c) * BUCKETS + self.half * NZ + o, 1)

    def index_row(self, c, x, o):
        return ((c * NX + x) * NZ + o) * LANES

    def fetch(self, source_row, count, shift, target_ref, start):
        def some(j, unused):
            source = source_row + j * UNROLL
            target = pl.multiple_of(start + j * UNROLL, UNROLL)
            for u in range(UNROLL):
                target_ref[pl.ds(target + u, 1), :] = self.pooled_ref[
                    pl.ds(self.index_ref[source + u] + shift, 1), :
                ]
            return unused

        lax.fori_loop(0, (count + (UNROLL - 1)) // UNROLL, some, 0)

    def gather(self, x, spilled):
        self.index_copy(0, x).wait()

        def bucket_step(o, spilled):
            row = self.index_row(0, x, o)
            count = self.index_ref[row + USED]
            start = (o * NX + x) * LANES
            self.fetch(row, jnp.minimum(count, USED), x * (FEAT * SAMP), self.group_ref, start)
            self.spilled_ref[spilled] = o * NX + x
            return spilled + (count > USED).astype(I32)

        return lax.fori_loop(0, NZ, bucket_step, spilled)

    def finish(self, spilled):
        blank = jnp.zeros((8 - NX, LANES), F32)
        for o in range(NZ):
            rows = jnp.concatenate(
                [self.row_ref[self.vector_row(0, x, o), :] for x in range(NX)], axis=1
            )
            weights = [self.weight_ref[self.vector_row(0, x, o), :] for x in range(NX)]
            columns = jnp.concatenate([*weights, blank], axis=0).T
            values = []
            for x in range(NX):
                start = (o * NX + x) * LANES
                values.append(self.group_ref[start : start + LANES, :] * columns[:, x : x + 1])
            values = jnp.concatenate(values, axis=0).astype(BF)
            self.total_ref[o] = jnp.dot(chosen(rows), values, preferred_element_type=F32)
        for c in range(1, CHUNKS):
            for x in range(NX):
                self.index_copy(c, x).wait()

        def spill_step(k, unused):
            i = self.spilled_ref[k]
            x, o = i & (NX - 1), i >> 2
            count = self.index_ref[self.index_row(0, x, o) + USED]

            def chunk_step(c, unused):
                rest = jnp.minimum(count - c * USED, USED)
                self.fetch(self.index_row(c, x, o), rest, x * (FEAT * SAMP), self.spill_ref, 0)
                weight = self.weight_ref[self.vector_row(c, x, o), :]
                column = jnp.broadcast_to(weight, (8, LANES)).T[:, :1]
                self.total_ref[o] += jnp.dot(
                    chosen(self.row_ref[self.vector_row(c, x, o), :]),
                    (self.spill_ref[...] * column).astype(BF),
                    preferred_element_type=F32,
                )
                return unused

            return lax.fori_loop(1, (count + (USED - 1)) // USED, chunk_step, unused)

        lax.fori_loop(0, spilled, spill_step, 0)
        self.out_ref[...] = self.total_ref[...].astype(BF)


UP_STEP = 1024
UP_STEPS = TIN // UP_STEP
UP_PART = 512


def pooled_kernel(
    me_ref,
    grad_ref,
    hidden0_ref,
    hidden1_ref,
    hidden2_ref,
    hidden3_ref,
    down_ref,
    up_hbm_ref,
    pooled_hbm_ref,
    pooled_ref,
    hid_ref,
    up_ref,
    up_sems,
    pooled_sems,
):
    def up_copy(k):
        rows = pl.ds(pl.multiple_of(k * UP_STEP, UP_STEP), UP_STEP)
        return pltpu.make_async_copy(up_hbm_ref.at[rows], up_ref.at[rows], up_sems.at[k])

    def pooled_copy(k, x):
        start = x * FEAT * SAMP + k * UP_STEP // E * SAMP
        rows = pl.ds(pl.multiple_of(start, UP_STEP), UP_STEP)
        return pltpu.make_async_copy(
            pooled_ref.at[rows], pooled_hbm_ref.at[rows], pooled_sems.at[k, x]
        )

    for k in range(UP_STEPS):
        up_copy(k).start()
    for r, hidden_ref in enumerate((hidden0_ref, hidden1_ref, hidden2_ref, hidden3_ref)):
        x = me_ref[0] ^ r
        backward = lax.dot_general(grad_ref[x], down_ref[...], NT, preferred_element_type=F32)
        keep = hidden_ref[...].astype(F32) > 0
        there = pl.ds(pl.multiple_of(x * SAMP, SAMP), SAMP)
        hid_ref[there, :] = jnp.where(keep, backward, 0.0).astype(BF)

    def up_step(k, unused):
        up_copy(k).wait()
        for j in range(UP_STEP // UP_PART):
            rows = pl.ds(pl.multiple_of(k * UP_STEP + j * UP_PART, UP_PART), UP_PART)
            result = lax.dot_general(
                hid_ref[...], up_ref[rows, :], NT, preferred_element_type=F32
            )
            result = result.astype(BF).astype(F32)
            for x in range(NX):
                for i in range(UP_PART // E):
                    block = (k * UP_STEP + j * UP_PART) // E + i
                    start = pl.multiple_of((x * FEAT + block) * SAMP, SAMP)
                    pooled_ref[pl.ds(start, SAMP), :] = result[
                        x * SAMP : (x + 1) * SAMP, i * E : (i + 1) * E
                    ]
        for x in range(NX):
            pooled_copy(k, x).start()
        return unused

    lax.fori_loop(0, UP_STEPS, up_step, 0)
    for k in range(UP_STEPS):
        for x in range(NX):
            pooled_copy(k, x).wait()


def pooled_gradients(me, grads, hiddens, down, up):
    hbm = pl.BlockSpec(memory_space=pltpu.HBM)
    vmem = pl.BlockSpec(memory_space=pltpu.VMEM)
    return pl.pallas_call(
        pooled_kernel,
        out_shape=pltpu.HBM((NX * FEAT * SAMP, E), F32),
        in_specs=[pl.BlockSpec(memory_space=pltpu.SMEM), *[vmem] * (NX + 2), hbm],
        out_specs=hbm,
        scratch_shapes=[
            pltpu.VMEM((NX * FEAT * SAMP, E), F32),
            pltpu.VMEM((NX * SAMP, HID), BF),
            pltpu.VMEM((TIN, HID), BF),
            pltpu.SemaphoreType.DMA((UP_STEPS,)),
            pltpu.SemaphoreType.DMA((UP_STEPS, NX)),
        ],
        compiler_params=pltpu.CompilerParams(vmem_limit_bytes=32 << 20),
        cost_estimate=pl.CostEstimate(flops=5 << 30, bytes_accessed=20 << 20, transcendentals=0),
    )(me, grads, *hiddens, down, in_hbm(up))


def table_kernel(
    half,
    index_hbm_ref,
    weight_ref,
    row_ref,
    pooled_hbm_ref,
    out_ref,
    pooled_ref,
    pooled_sems,
    *scratch,
):
    table = Table(half, index_hbm_ref, weight_ref, row_ref, pooled_ref, out_ref, scratch)

    def pooled_copy(x):
        rows = pl.ds(x * FEAT * SAMP, FEAT * SAMP)
        return pltpu.make_async_copy(
            pooled_hbm_ref.at[rows], pooled_ref.at[rows], pooled_sems.at[x]
        )

    for x in range(NX):
        pooled_copy(x).start()
    table.begin()
    spilled = 0
    for x in range(NX):
        pooled_copy(x).wait()
        spilled = table.gather(x, spilled)
    table.finish(spilled)


def half_tables(half, index, weight, rows, pooled):
    hbm = pl.BlockSpec(memory_space=pltpu.HBM)
    vmem = pl.BlockSpec(memory_space=pltpu.VMEM)
    return pl.pallas_call(
        functools.partial(table_kernel, half),
        out_shape=jax.ShapeDtypeStruct((NZ, HALF, E), BF),
        in_specs=[hbm, vmem, vmem, hbm],
        out_specs=vmem,
        scratch_shapes=[
            pltpu.VMEM((NX * FEAT * SAMP, E), F32),
            pltpu.SemaphoreType.DMA((NX,)),
            *TABLE_SCRATCH,
        ],
        compiler_params=pltpu.CompilerParams(vmem_limit_bytes=32 << 20),
        cost_estimate=pl.CostEstimate(flops=5 << 30, bytes_accessed=10 << 20, transcendentals=0),
    )(in_hbm(index), weight, rows, in_hbm(pooled))


def local(
    out_grad,
    hidden_pre,
    down_proj,
    up_proj,
    feature_slot,
    element_segment,
    element_weight,
    row_owner,
    row_local,
):
    own = hidden_pre[0]
    hiddens = [own] + [
        lax.ppermute(own, "x", [(i, i ^ r) for i in range(NX)]) for r in range(1, NX)
    ]
    by_tower = jnp.transpose(out_grad, (1, 0, 2))
    grads = lax.all_to_all(
        jnp.broadcast_to(by_tower, (NX, *by_tower.shape)).reshape(-1, *by_tower.shape[1:]),
        ("x", "tower"),
        split_axis=0,
        concat_axis=0,
        tiled=True,
    ).reshape(NX, SAMP, TOUT)
    swap_x = functools.partial(
        lax.all_to_all, axis_name="x", split_axis=0, concat_axis=0, tiled=True
    )
    flat = (1, ELEMS)
    buckets = bucket_elements(
        element_segment.reshape(flat),
        element_weight.reshape(flat),
        row_owner.reshape(flat),
        row_local.reshape(flat),
        feature_slot,
        grads,
    )
    parts = swap_x(buckets).reshape(NX, PIECES, CHUNKS * BUCKETS, LANES).astype(F32)
    index = (parts[:, 0] * SAMP + parts[:, 1]).astype(I32).reshape(-1)
    rows = parts[:, 2].astype(I32).reshape(NX * CHUNKS * BUCKETS, LANES)
    weight = (parts[:, 3] + parts[:, 4]).reshape(NX * CHUNKS * BUCKETS, LANES)
    me = lax.axis_index("x").astype(I32).reshape(1)
    pooled = pooled_gradients(me, grads, hiddens, down_proj[0], up_proj[0])
    swap = functools.partial(
        lax.all_to_all, axis_name="z", split_axis=0, concat_axis=0, tiled=True
    )
    first = swap(half_tables(0, index, weight, rows, pooled))
    second = swap(half_tables(1, index, weight, rows, pooled))
    table_grad = jnp.concatenate(
        [jnp.sum(first.astype(F32), axis=0), jnp.sum(second.astype(F32), axis=0)], axis=0
    )
    return table_grad.reshape(1, ROW_DEV, E)


def solution(mesh):
    towers = mesh.shape["tower"]
    grid = Mesh(mesh.devices.reshape(towers, NZ, NX), ("tower", "z", "x"))
    shard = ("z", "x")
    in_specs = (
        P(("tower", "z", "x"), None, None),
        P("tower", shard, None),
        P("tower", None, None),
        P("tower", None, None),
        P("tower", None),
        P("tower", shard, None),
        P("tower", shard, None),
        P("tower", shard, None, None),
        P("tower", shard, None),
    )
    out_specs = P("tower", shard, None)
    return jax.shard_map(local, mesh=grid, in_specs=in_specs, out_specs=out_specs, check_vma=False)
```

```python
import functools

import jax
import jax.numpy as jnp
from jax import lax
from jax.experimental import pallas as pl
from jax.experimental.pallas import tpu as pltpu
from jax.sharding import Mesh
from jax.sharding import PartitionSpec as P

E = 128
FEAT = 32
SAMP = 128
HID = 1024
TOUT = 256
TIN = 4096
ROW_DEV = 512
ELEMS = 5120
CAP = 320
NX = 4
NZ = 8
HALVES = 2
HALF = ROW_DEV // HALVES
BUCKETS = NZ * HALVES
SUBS = NX * BUCKETS
PIECES = 5
SLOTS = 384
LANES = 128
CHUNKS = SLOTS // LANES
USED = 120
STEP = 512
UNROLL = 16
BATCH = 4
BF = jnp.bfloat16
F32 = jnp.float32
I32 = jnp.int32
NT = (((1,), (1,)), ((), ()))


def in_hbm(operand):
    return pltpu.with_memory_space_constraint(operand, pltpu.HBM)


def bucket_kernel(
    seg_ref,
    weight_ref,
    owner_ref,
    row_ref,
    slot_ref,
    after_ref,
    out_ref,
    acc_ref,
):
    del after_ref
    square = (FEAT, FEAT)
    diagonal = lax.broadcasted_iota(I32, square, 0) == lax.broadcasted_iota(I32, square, 1)
    slots = jnp.sum(
        jnp.where(diagonal, slot_ref[...].astype(F32), 0.0), axis=1, keepdims=True
    )
    upper = (
        lax.broadcasted_iota(I32, (STEP, STEP), 0) <= lax.broadcasted_iota(I32, (STEP, STEP), 1)
    ).astype(F32).astype(BF)
    sub_ids = lax.broadcasted_iota(I32, (SUBS, STEP), 0)
    feat_ids = lax.broadcasted_iota(I32, (FEAT, STEP), 0)
    most = (CHUNKS - 1) * LANES
    slot_ids = lax.broadcasted_iota(I32, (most, STEP), 0).astype(F32)
    acc_ref[...] = jnp.zeros_like(acc_ref)

    def step(k, carry, first=0, width=most):
        cols = pl.ds(pl.multiple_of(k * STEP, STEP), STEP)
        seg = seg_ref[:, cols]
        weight = weight_ref[:, cols]
        owner = owner_ref[:, cols]
        row = row_ref[:, cols]
        sub = (owner & 3) * BUCKETS + (row >> 8) * NZ + (owner >> 2)
        mine = sub_ids == sub
        ones = jnp.where(mine, 1.0, 0.0)
        inclusive = jnp.dot(ones.astype(BF), upper, preferred_element_type=F32) + carry
        rank = jnp.sum(ones * inclusive, axis=0, keepdims=True) - 1.0
        block = jnp.sum(
            jnp.where(feat_ids == (seg & 31), slots, 0.0), axis=0, keepdims=True
        )
        sample = (seg >> 5).astype(F32)
        row_next = ((row & 255) + 1).astype(F32)
        high = weight.astype(BF).astype(F32)
        rest = weight - high
        middle = rest.astype(BF).astype(F32)
        pieces = (block, sample, row_next, high, middle)
        left = jnp.concatenate([(ones * piece).astype(BF) for piece in pieces], axis=0)
        place = rank
        for c in range(1, CHUNKS):
            place = place + jnp.where(rank >= c * USED, float(LANES - USED), 0.0)
        right = jnp.where(slot_ids[:width] == place - first, 1.0, 0.0).astype(BF)
        acc_ref[:, first : first + width] += lax.dot_general(
            left, right, NT, preferred_element_type=F32
        )
        return inclusive[:, STEP - 1 : STEP]

    nothing = jnp.zeros((SUBS, 1), F32)
    count = lax.fori_loop(0, ELEMS // STEP, step, nothing, unroll=10)

    @pl.when(jnp.max(count) > (CHUNKS - 1) * USED)
    def _():
        last = functools.partial(step, first=most, width=LANES)
        lax.fori_loop(0, ELEMS // STEP, last, nothing)

    count = jnp.broadcast_to(count.astype(I32), (SUBS, LANES))
    count_parts = ((count >> 7).astype(F32), (count & 127).astype(F32))
    spare = lax.broadcasted_iota(I32, (SUBS, LANES), 1) >= USED
    for p in range(PIECES):
        for c in range(CHUNKS):
            part = acc_ref[p * SUBS : (p + 1) * SUBS, c * LANES : (c + 1) * LANES]
            if p < 2 and c == 0:
                part = jnp.where(spare, count_parts[p], part)
            part = part.astype(BF)
            for x in range(NX):
                out_ref[x, p, c] = part[x * BUCKETS : (x + 1) * BUCKETS]


def bucket_elements(segment, weight, owner, row, slots, after):
    vmem = pl.BlockSpec(memory_space=pltpu.VMEM)
    operands = (segment, weight, owner, row, slots)
    return pl.pallas_call(
        bucket_kernel,
        out_shape=jax.ShapeDtypeStruct((NX, PIECES, CHUNKS, BUCKETS, LANES), BF),
        in_specs=[vmem] * 5 + [pl.BlockSpec(memory_space=pl.ANY)],
        out_specs=vmem,
        scratch_shapes=[pltpu.VMEM((PIECES * SUBS, SLOTS), F32)],
        compiler_params=pltpu.CompilerParams(vmem_limit_bytes=24 << 20),
        cost_estimate=pl.CostEstimate(flops=3 << 30, bytes_accessed=1 << 20, transcendentals=0),
    )(*[in_hbm(operand) for operand in operands], after)


def chosen(rows):
    row_ids = lax.broadcasted_iota(I32, (HALF, rows.shape[1]), 0) + 1
    return jnp.where(row_ids == rows, 1.0, 0.0).astype(BF)


TABLE_SCRATCH = (
    pltpu.VMEM((NZ * NX * LANES, E), F32),
    pltpu.VMEM((BATCH * LANES, E), F32),
    pltpu.VMEM((NZ, HALF, E), F32),
    pltpu.VMEM((NZ * NX * LANES, E), F32),
    pltpu.SMEM((CHUNKS * NX * NZ * LANES,), I32),
    pltpu.SMEM((CHUNKS * NX * NZ,), I32),
    pltpu.SemaphoreType.DMA((CHUNKS, NX)),
)


class Table:
    def __init__(
        self, half, index_hbm_ref, weight_ref, row_ref, pooled_ref, out_ref, scratch
    ):
        self.half = half
        self.pooled_ref = pooled_ref
        self.index_hbm_ref, self.weight_ref, self.row_ref = index_hbm_ref, weight_ref, row_ref
        self.out_ref = out_ref
        self.group_ref, self.spill_ref, self.total_ref, self.scale_ref = scratch[:4]
        self.index_ref, self.spilled_ref, self.index_sems = scratch[4:]

    def index_copy(self, c, x):
        part = NZ * LANES
        start = ((x * CHUNKS + c) * BUCKETS + self.half * NZ) * LANES
        return pltpu.make_async_copy(
            self.index_hbm_ref.at[pl.ds(start, part)],
            self.index_ref.at[pl.ds((c * NX + x) * part, part)],
            self.index_sems.at[c, x],
        )

    def begin(self):
        for c in range(CHUNKS):
            for x in range(NX):
                self.index_copy(c, x).start()
        self.group_ref[...] = jnp.zeros_like(self.group_ref)
        self.spill_ref[...] = jnp.zeros_like(self.spill_ref)
        blank = jnp.zeros((8 - NX, LANES), F32)
        for o in range(NZ):
            weights = [self.weight_ref[self.vector_row(0, x, o), :] for x in range(NX)]
            columns = jnp.concatenate([*weights, blank], axis=0).T
            for x in range(NX):
                start = (o * NX + x) * LANES
                self.scale_ref[start : start + LANES, :] = jnp.broadcast_to(
                    columns[:, x : x + 1], (LANES, E)
                )

    def vector_row(self, c, x, o):
        return pl.ds((x * CHUNKS + c) * BUCKETS + self.half * NZ + o, 1)

    def index_row(self, c, x, o):
        return ((c * NX + x) * NZ + o) * LANES

    def fetch(self, source_row, count, shift, target_ref, start):
        def some(j, unused):
            source = source_row + j * UNROLL
            target = pl.multiple_of(start + j * UNROLL, UNROLL)
            for u in range(UNROLL):
                target_ref[pl.ds(target + u, 1), :] = self.pooled_ref[
                    pl.ds(self.index_ref[source + u] + shift, 1), :
                ]
            return unused

        lax.fori_loop(0, (count + (UNROLL - 1)) // UNROLL, some, 0)

    def gather(self, x, spilled):
        self.index_copy(0, x).wait()

        def bucket_step(o, spilled):
            row = self.index_row(0, x, o)
            count = self.index_ref[row + USED]
            start = (o * NX + x) * LANES
            self.fetch(row, jnp.minimum(count, USED), x * (FEAT * SAMP), self.group_ref, start)
            for c in range(1, CHUNKS):
                self.spilled_ref[spilled] = (c * NZ + o) * NX + x
                spilled = spilled + (count > c * USED).astype(I32)
            return spilled

        return lax.fori_loop(0, NZ, bucket_step, spilled)

    def finish(self, spilled):
        for o in range(NZ):
            rows = jnp.concatenate(
                [self.row_ref[self.vector_row(0, x, o), :] for x in range(NX)], axis=1
            )
            these = slice(o * NX * LANES, (o + 1) * NX * LANES)
            values = (self.group_ref[these, :] * self.scale_ref[these, :]).astype(BF)
            self.total_ref[o] = jnp.dot(chosen(rows), values, preferred_element_type=F32)
        for c in range(1, CHUNKS):
            for x in range(NX):
                self.index_copy(c, x).wait()

        def spill_step(k, unused):
            entries = []
            for q in range(BATCH):
                number = k * BATCH + q
                entry = self.spilled_ref[jnp.minimum(number, spilled - 1)]
                x, o = entry & (NX - 1), (entry >> 2) & (NZ - 1)
                c = entry >> 5
                count = self.index_ref[self.index_row(0, x, o) + USED] - c * USED
                count = jnp.where(number < spilled, jnp.minimum(count, USED), 0)
                shift = x * (FEAT * SAMP)
                self.fetch(self.index_row(c, x, o), count, shift, self.spill_ref, q * LANES)
                entries.append((x, o, c, count))
            for q, (x, o, c, count) in enumerate(entries):
                row = self.vector_row(c, x, o)
                weight = jnp.where(count > 0, self.weight_ref[row, :], 0.0)
                column = jnp.broadcast_to(weight, (8, LANES)).T[:, :1]
                values = self.spill_ref[q * LANES : (q + 1) * LANES, :] * column
                self.total_ref[o] += jnp.dot(
                    chosen(self.row_ref[row, :]),
                    values.astype(BF),
                    preferred_element_type=F32,
                )
            return unused

        lax.fori_loop(0, (spilled + (BATCH - 1)) // BATCH, spill_step, 0)
        self.out_ref[...] = self.total_ref[...].astype(BF)


UP_STEP = 1024
UP_STEPS = TIN // UP_STEP
UP_PART = 512


def pooled_kernel(
    me_ref,
    grad_ref,
    hidden0_ref,
    hidden1_ref,
    hidden2_ref,
    hidden3_ref,
    down_ref,
    up_hbm_ref,
    pooled_hbm_ref,
    pooled_ref,
    hid_ref,
    up_ref,
    up_sems,
    pooled_sems,
):
    def up_copy(k):
        rows = pl.ds(pl.multiple_of(k * UP_STEP, UP_STEP), UP_STEP)
        return pltpu.make_async_copy(up_hbm_ref.at[rows], up_ref.at[rows], up_sems.at[k])

    def pooled_copy(k, x):
        start = x * FEAT * SAMP + k * UP_STEP // E * SAMP
        rows = pl.ds(pl.multiple_of(start, UP_STEP), UP_STEP)
        return pltpu.make_async_copy(
            pooled_ref.at[rows], pooled_hbm_ref.at[rows], pooled_sems.at[k, x]
        )

    for k in range(UP_STEPS):
        up_copy(k).start()
    for r, hidden_ref in enumerate((hidden0_ref, hidden1_ref, hidden2_ref, hidden3_ref)):
        x = me_ref[0] ^ r
        backward = lax.dot_general(grad_ref[x], down_ref[...], NT, preferred_element_type=F32)
        keep = hidden_ref[...].astype(F32) > 0
        there = pl.ds(pl.multiple_of(x * SAMP, SAMP), SAMP)
        hid_ref[there, :] = jnp.where(keep, backward, 0.0).astype(BF)

    def up_step(k, unused):
        up_copy(k).wait()
        for j in range(UP_STEP // UP_PART):
            rows = pl.ds(pl.multiple_of(k * UP_STEP + j * UP_PART, UP_PART), UP_PART)
            result = lax.dot_general(
                hid_ref[...], up_ref[rows, :], NT, preferred_element_type=F32
            )
            result = result.astype(BF).astype(F32)
            for x in range(NX):
                for i in range(UP_PART // E):
                    block = (k * UP_STEP + j * UP_PART) // E + i
                    start = pl.multiple_of((x * FEAT + block) * SAMP, SAMP)
                    pooled_ref[pl.ds(start, SAMP), :] = result[
                        x * SAMP : (x + 1) * SAMP, i * E : (i + 1) * E
                    ]
        for x in range(NX):
            pooled_copy(k, x).start()
        return unused

    lax.fori_loop(0, UP_STEPS, up_step, 0)
    for k in range(UP_STEPS):
        for x in range(NX):
            pooled_copy(k, x).wait()


def pooled_gradients(me, grads, hiddens, down, up):
    hbm = pl.BlockSpec(memory_space=pltpu.HBM)
    vmem = pl.BlockSpec(memory_space=pltpu.VMEM)
    return pl.pallas_call(
        pooled_kernel,
        out_shape=pltpu.HBM((NX * FEAT * SAMP, E), F32),
        in_specs=[pl.BlockSpec(memory_space=pltpu.SMEM), *[vmem] * (NX + 2), hbm],
        out_specs=hbm,
        scratch_shapes=[
            pltpu.VMEM((NX * FEAT * SAMP, E), F32),
            pltpu.VMEM((NX * SAMP, HID), BF),
            pltpu.VMEM((TIN, HID), BF),
            pltpu.SemaphoreType.DMA((UP_STEPS,)),
            pltpu.SemaphoreType.DMA((UP_STEPS, NX)),
        ],
        compiler_params=pltpu.CompilerParams(vmem_limit_bytes=32 << 20),
        cost_estimate=pl.CostEstimate(flops=5 << 30, bytes_accessed=20 << 20, transcendentals=0),
    )(me, grads, *hiddens, down, in_hbm(up))


def table_kernel(
    half,
    index_hbm_ref,
    weight_ref,
    row_ref,
    pooled_hbm_ref,
    out_ref,
    pooled_ref,
    pooled_sems,
    *scratch,
):
    table = Table(half, index_hbm_ref, weight_ref, row_ref, pooled_ref, out_ref, scratch)

    def pooled_copy(x):
        rows = pl.ds(x * FEAT * SAMP, FEAT * SAMP)
        return pltpu.make_async_copy(
            pooled_hbm_ref.at[rows], pooled_ref.at[rows], pooled_sems.at[x]
        )

    for x in range(NX):
        pooled_copy(x).start()
    table.begin()
    spilled = 0
    for x in range(NX):
        pooled_copy(x).wait()
        spilled = table.gather(x, spilled)
    table.finish(spilled)


def half_tables(half, index, weight, rows, pooled):
    hbm = pl.BlockSpec(memory_space=pltpu.HBM)
    vmem = pl.BlockSpec(memory_space=pltpu.VMEM)
    return pl.pallas_call(
        functools.partial(table_kernel, half),
        out_shape=jax.ShapeDtypeStruct((NZ, HALF, E), BF),
        in_specs=[hbm, vmem, vmem, hbm],
        out_specs=vmem,
        scratch_shapes=[
            pltpu.VMEM((NX * FEAT * SAMP, E), F32),
            pltpu.SemaphoreType.DMA((NX,)),
            *TABLE_SCRATCH,
        ],
        compiler_params=pltpu.CompilerParams(vmem_limit_bytes=32 << 20),
        cost_estimate=pl.CostEstimate(flops=5 << 30, bytes_accessed=10 << 20, transcendentals=0),
    )(in_hbm(index), weight, rows, in_hbm(pooled))


def local(
    out_grad,
    hidden_pre,
    down_proj,
    up_proj,
    feature_slot,
    element_segment,
    element_weight,
    row_owner,
    row_local,
):
    own = hidden_pre[0]
    hiddens = [own] + [
        lax.ppermute(own, "x", [(i, i ^ r) for i in range(NX)]) for r in range(1, NX)
    ]
    by_tower = jnp.transpose(out_grad, (1, 0, 2))
    grads = lax.all_to_all(
        jnp.broadcast_to(by_tower, (NX, *by_tower.shape)).reshape(-1, *by_tower.shape[1:]),
        ("x", "tower"),
        split_axis=0,
        concat_axis=0,
        tiled=True,
    ).reshape(NX, SAMP, TOUT)
    swap_x = functools.partial(
        lax.all_to_all, axis_name="x", split_axis=0, concat_axis=0, tiled=True
    )
    flat = (1, ELEMS)
    buckets = bucket_elements(
        element_segment.reshape(flat),
        element_weight.reshape(flat),
        row_owner.reshape(flat),
        row_local.reshape(flat),
        feature_slot,
        grads,
    )
    parts = swap_x(buckets).reshape(NX, PIECES, CHUNKS * BUCKETS, LANES).astype(F32)
    index = (parts[:, 0] * SAMP + parts[:, 1]).astype(I32).reshape(-1)
    rows = parts[:, 2].astype(I32).reshape(NX * CHUNKS * BUCKETS, LANES)
    weight = (parts[:, 3] + parts[:, 4]).reshape(NX * CHUNKS * BUCKETS, LANES)
    me = lax.axis_index("x").astype(I32).reshape(1)
    pooled = pooled_gradients(me, grads, hiddens, down_proj[0], up_proj[0])
    swap = functools.partial(
        lax.all_to_all, axis_name="z", split_axis=0, concat_axis=0, tiled=True
    )
    first = swap(half_tables(0, index, weight, rows, pooled))
    second = swap(half_tables(1, index, weight, rows, pooled))
    table_grad = jnp.concatenate(
        [jnp.sum(first.astype(F32), axis=0), jnp.sum(second.astype(F32), axis=0)], axis=0
    )
    return table_grad.reshape(1, ROW_DEV, E)


def solution(mesh):
    towers = mesh.shape["tower"]
    grid = Mesh(mesh.devices.reshape(towers, NZ, NX), ("tower", "z", "x"))
    shard = ("z", "x")
    in_specs = (
        P(("tower", "z", "x"), None, None),
        P("tower", shard, None),
        P("tower", None, None),
        P("tower", None, None),
        P("tower", None),
        P("tower", shard, None),
        P("tower", shard, None),
        P("tower", shard, None, None),
        P("tower", shard, None),
    )
    out_specs = P("tower", shard, None)
    return jax.shard_map(local, mesh=grid, in_specs=in_specs, out_specs=out_specs, check_vma=False)
```

```python
import functools

import jax
import jax.numpy as jnp
from jax import lax
from jax.experimental import pallas as pl
from jax.experimental.pallas import tpu as pltpu
from jax.sharding import Mesh
from jax.sharding import PartitionSpec as P

E = 128
FEAT = 32
SAMP = 128
HID = 1024
TOUT = 256
TIN = 4096
ROW_DEV = 512
ELEMS = 5120
CAP = 320
NX = 4
NZ = 8
HALVES = 2
HALF = ROW_DEV // HALVES
BUCKETS = NZ * HALVES
SUBS = NX * BUCKETS
PIECES = 5
SLOTS = 384
LANES = 128
CHUNKS = SLOTS // LANES
USED = 120
STEP = 512
UNROLL = 16
BATCH = 4
BF = jnp.bfloat16
F32 = jnp.float32
I32 = jnp.int32
NT = (((1,), (1,)), ((), ()))


def in_hbm(operand):
    return pltpu.with_memory_space_constraint(operand, pltpu.HBM)


def bucket_kernel(
    seg_ref,
    weight_ref,
    owner_ref,
    row_ref,
    slot_ref,
    after_ref,
    out_ref,
    acc_ref,
):
    del after_ref
    square = (FEAT, FEAT)
    diagonal = lax.broadcasted_iota(I32, square, 0) == lax.broadcasted_iota(I32, square, 1)
    slots = jnp.sum(
        jnp.where(diagonal, slot_ref[...].astype(F32), 0.0), axis=1, keepdims=True
    )
    upper = (
        lax.broadcasted_iota(I32, (STEP, STEP), 0) <= lax.broadcasted_iota(I32, (STEP, STEP), 1)
    ).astype(F32).astype(BF)
    sub_ids = lax.broadcasted_iota(I32, (SUBS, STEP), 0)
    feat_ids = lax.broadcasted_iota(I32, (FEAT, STEP), 0)
    most = (CHUNKS - 1) * LANES
    slot_ids = lax.broadcasted_iota(I32, (most, STEP), 0).astype(F32)
    acc_ref[...] = jnp.zeros_like(acc_ref)

    def step(k, carry, first=0, width=most):
        cols = pl.ds(pl.multiple_of(k * STEP, STEP), STEP)
        seg = seg_ref[:, cols]
        weight = weight_ref[:, cols]
        owner = owner_ref[:, cols]
        row = row_ref[:, cols]
        sub = (owner & 3) * BUCKETS + (row >> 8) * NZ + (owner >> 2)
        mine = sub_ids == sub
        ones = jnp.where(mine, 1.0, 0.0)
        inclusive = jnp.dot(ones.astype(BF), upper, preferred_element_type=F32) + carry
        rank = jnp.sum(ones * inclusive, axis=0, keepdims=True) - 1.0
        block = jnp.sum(
            jnp.where(feat_ids == (seg & 31), slots, 0.0), axis=0, keepdims=True
        )
        sample = (seg >> 5).astype(F32)
        row_next = ((row & 255) + 1).astype(F32)
        high = weight.astype(BF).astype(F32)
        rest = weight - high
        middle = rest.astype(BF).astype(F32)
        pieces = (block, sample, row_next, high, middle)
        left = jnp.concatenate([(ones * piece).astype(BF) for piece in pieces], axis=0)
        place = rank
        for c in range(1, CHUNKS):
            place = place + jnp.where(rank >= c * USED, float(LANES - USED), 0.0)
        right = jnp.where(slot_ids[:width] == place - first, 1.0, 0.0).astype(BF)
        acc_ref[:, first : first + width] += lax.dot_general(
            left, right, NT, preferred_element_type=F32
        )
        return inclusive[:, STEP - 1 : STEP]

    nothing = jnp.zeros((SUBS, 1), F32)
    count = lax.fori_loop(0, ELEMS // STEP, step, nothing, unroll=10)

    @pl.when(jnp.max(count) > (CHUNKS - 1) * USED)
    def _():
        last = functools.partial(step, first=most, width=LANES)
        lax.fori_loop(0, ELEMS // STEP, last, nothing)

    count = jnp.broadcast_to(count.astype(I32), (SUBS, LANES))
    count_parts = ((count >> 7).astype(F32), (count & 127).astype(F32))
    spare = lax.broadcasted_iota(I32, (SUBS, LANES), 1) >= USED
    for p in range(PIECES):
        for c in range(CHUNKS):
            part = acc_ref[p * SUBS : (p + 1) * SUBS, c * LANES : (c + 1) * LANES]
            if p < 2 and c == 0:
                part = jnp.where(spare, count_parts[p], part)
            part = part.astype(BF)
            for x in range(NX):
                out_ref[x, p, c] = part[x * BUCKETS : (x + 1) * BUCKETS]


def bucket_elements(segment, weight, owner, row, slots, after):
    vmem = pl.BlockSpec(memory_space=pltpu.VMEM)
    operands = (segment, weight, owner, row, slots)
    return pl.pallas_call(
        bucket_kernel,
        out_shape=jax.ShapeDtypeStruct((NX, PIECES, CHUNKS, BUCKETS, LANES), BF),
        in_specs=[vmem] * 5 + [pl.BlockSpec(memory_space=pl.ANY)],
        out_specs=vmem,
        scratch_shapes=[pltpu.VMEM((PIECES * SUBS, SLOTS), F32)],
        compiler_params=pltpu.CompilerParams(vmem_limit_bytes=24 << 20),
        cost_estimate=pl.CostEstimate(flops=3 << 30, bytes_accessed=1 << 20, transcendentals=0),
    )(*[in_hbm(operand) for operand in operands], after)


def chosen(rows):
    row_ids = lax.broadcasted_iota(I32, (HALF, rows.shape[1]), 0) + 1
    return jnp.where(row_ids == rows, 1.0, 0.0).astype(BF)


TABLE_SCRATCH = (
    pltpu.VMEM((NZ * NX * LANES, E), F32),
    pltpu.VMEM((BATCH * LANES, E), F32),
    pltpu.VMEM((NZ, HALF, E), F32),
    pltpu.VMEM((NZ * NX * LANES, E), F32),
    pltpu.VMEM((NX * CHUNKS * BUCKETS, LANES), I32),
    pltpu.VMEM((NX * CHUNKS * BUCKETS, LANES), I32),
    pltpu.VMEM((NX * CHUNKS * BUCKETS, LANES), F32),
    pltpu.SMEM((CHUNKS * NX * NZ, LANES), I32),
    pltpu.SMEM((CHUNKS * NX * NZ,), I32),
    pltpu.SemaphoreType.DMA((CHUNKS, NX)),
)


class Table:
    def __init__(self, half, parts_ref, pooled_ref, out_ref, scratch):
        self.half = half
        self.parts_ref, self.pooled_ref, self.out_ref = parts_ref, pooled_ref, out_ref
        self.group_ref, self.spill_ref, self.total_ref, self.scale_ref = scratch[:4]
        self.place_ref, self.row_ref, self.weight_ref = scratch[4:7]
        self.index_ref, self.spilled_ref, self.index_sems = scratch[7:]

    def index_copy(self, c, x):
        start = (x * CHUNKS + c) * BUCKETS + self.half * NZ
        return pltpu.make_async_copy(
            self.place_ref.at[pl.ds(start, NZ)],
            self.index_ref.at[pl.ds((c * NX + x) * NZ, NZ)],
            self.index_sems.at[c, x],
        )

    def begin(self):
        for x in range(NX):
            block, sample, row, high, middle = [
                self.parts_ref[x, p].astype(F32) for p in range(PIECES)
            ]
            these = slice(x * CHUNKS * BUCKETS, (x + 1) * CHUNKS * BUCKETS)
            self.place_ref[these, :] = (block * SAMP + sample).astype(I32)
            self.row_ref[these, :] = row.astype(I32)
            self.weight_ref[these, :] = high + middle
        for c in range(CHUNKS):
            for x in range(NX):
                self.index_copy(c, x).start()
        self.group_ref[...] = jnp.zeros_like(self.group_ref)
        self.spill_ref[...] = jnp.zeros_like(self.spill_ref)
        blank = jnp.zeros((8 - NX, LANES), F32)
        for o in range(NZ):
            weights = [self.weight_ref[self.vector_row(0, x, o), :] for x in range(NX)]
            columns = jnp.concatenate([*weights, blank], axis=0).T
            for x in range(NX):
                start = (o * NX + x) * LANES
                self.scale_ref[start : start + LANES, :] = jnp.broadcast_to(
                    columns[:, x : x + 1], (LANES, E)
                )

    def vector_row(self, c, x, o):
        return pl.ds((x * CHUNKS + c) * BUCKETS + self.half * NZ + o, 1)

    def index_row(self, c, x, o):
        return (c * NX + x) * NZ + o

    def fetch(self, source_row, count, shift, target_ref, start):
        places = self.index_ref.at[source_row]

        def some(j, unused):
            source = j * UNROLL
            target = pl.multiple_of(start + j * UNROLL, UNROLL)
            for u in range(UNROLL):
                target_ref[pl.ds(target + u, 1), :] = self.pooled_ref[
                    pl.ds(places[source + u] + shift, 1), :
                ]
            return unused

        lax.fori_loop(0, (count + (UNROLL - 1)) // UNROLL, some, 0)

    def gather(self, x, spilled):
        self.index_copy(0, x).wait()

        def bucket_step(o, spilled):
            row = self.index_row(0, x, o)
            count = self.index_ref[row, USED]
            start = (o * NX + x) * LANES
            self.fetch(row, jnp.minimum(count, USED), x * (FEAT * SAMP), self.group_ref, start)
            for c in range(1, CHUNKS):
                self.spilled_ref[spilled] = (c * NZ + o) * NX + x
                spilled = spilled + (count > c * USED).astype(I32)
            return spilled

        return lax.fori_loop(0, NZ, bucket_step, spilled)

    def finish(self, spilled):
        for o in range(NZ):
            rows = jnp.concatenate(
                [self.row_ref[self.vector_row(0, x, o), :] for x in range(NX)], axis=1
            )
            these = slice(o * NX * LANES, (o + 1) * NX * LANES)
            values = (self.group_ref[these, :] * self.scale_ref[these, :]).astype(BF)
            self.total_ref[o] = jnp.dot(chosen(rows), values, preferred_element_type=F32)
        for c in range(1, CHUNKS):
            for x in range(NX):
                self.index_copy(c, x).wait()

        def spill_step(k, unused):
            entries = []
            for q in range(BATCH):
                number = k * BATCH + q
                entry = self.spilled_ref[jnp.minimum(number, spilled - 1)]
                x, o = entry & (NX - 1), (entry >> 2) & (NZ - 1)
                c = entry >> 5
                count = self.index_ref[self.index_row(0, x, o), USED] - c * USED
                count = jnp.where(number < spilled, jnp.minimum(count, USED), 0)
                shift = x * (FEAT * SAMP)
                self.fetch(self.index_row(c, x, o), count, shift, self.spill_ref, q * LANES)
                entries.append((x, o, c, count))
            for q, (x, o, c, count) in enumerate(entries):
                row = self.vector_row(c, x, o)
                weight = jnp.where(count > 0, self.weight_ref[row, :], 0.0)
                column = jnp.broadcast_to(weight, (8, LANES)).T[:, :1]
                values = self.spill_ref[q * LANES : (q + 1) * LANES, :] * column
                self.total_ref[o] += jnp.dot(
                    chosen(self.row_ref[row, :]),
                    values.astype(BF),
                    preferred_element_type=F32,
                )
            return unused

        lax.fori_loop(0, (spilled + (BATCH - 1)) // BATCH, spill_step, 0)
        self.out_ref[...] = self.total_ref[...].astype(BF)


UP_STEP = 1024
UP_STEPS = TIN // UP_STEP
UP_PART = 512


def pooled_kernel(
    me_ref,
    grad_ref,
    hidden0_ref,
    hidden1_ref,
    hidden2_ref,
    hidden3_ref,
    down_ref,
    up_hbm_ref,
    pooled_hbm_ref,
    pooled_ref,
    hid_ref,
    up_ref,
    up_sems,
    pooled_sems,
):
    def up_copy(k):
        rows = pl.ds(pl.multiple_of(k * UP_STEP, UP_STEP), UP_STEP)
        return pltpu.make_async_copy(up_hbm_ref.at[rows], up_ref.at[rows], up_sems.at[k])

    def pooled_copy(k, x):
        start = x * FEAT * SAMP + k * UP_STEP // E * SAMP
        rows = pl.ds(pl.multiple_of(start, UP_STEP), UP_STEP)
        return pltpu.make_async_copy(
            pooled_ref.at[rows], pooled_hbm_ref.at[rows], pooled_sems.at[k, x]
        )

    for k in range(UP_STEPS):
        up_copy(k).start()
    for r, hidden_ref in enumerate((hidden0_ref, hidden1_ref, hidden2_ref, hidden3_ref)):
        x = me_ref[0] ^ r
        backward = lax.dot_general(grad_ref[x], down_ref[...], NT, preferred_element_type=F32)
        keep = hidden_ref[...].astype(F32) > 0
        there = pl.ds(pl.multiple_of(x * SAMP, SAMP), SAMP)
        hid_ref[there, :] = jnp.where(keep, backward, 0.0).astype(BF)

    def up_step(k, unused):
        up_copy(k).wait()
        for j in range(UP_STEP // UP_PART):
            rows = pl.ds(pl.multiple_of(k * UP_STEP + j * UP_PART, UP_PART), UP_PART)
            result = lax.dot_general(
                hid_ref[...], up_ref[rows, :], NT, preferred_element_type=F32
            )
            result = result.astype(BF).astype(F32)
            for x in range(NX):
                for i in range(UP_PART // E):
                    block = (k * UP_STEP + j * UP_PART) // E + i
                    start = pl.multiple_of((x * FEAT + block) * SAMP, SAMP)
                    pooled_ref[pl.ds(start, SAMP), :] = result[
                        x * SAMP : (x + 1) * SAMP, i * E : (i + 1) * E
                    ]
        for x in range(NX):
            pooled_copy(k, x).start()
        return unused

    lax.fori_loop(0, UP_STEPS, up_step, 0)
    for k in range(UP_STEPS):
        for x in range(NX):
            pooled_copy(k, x).wait()


def pooled_gradients(me, grads, hiddens, down, up):
    hbm = pl.BlockSpec(memory_space=pltpu.HBM)
    vmem = pl.BlockSpec(memory_space=pltpu.VMEM)
    return pl.pallas_call(
        pooled_kernel,
        out_shape=pltpu.HBM((NX * FEAT * SAMP, E), F32),
        in_specs=[pl.BlockSpec(memory_space=pltpu.SMEM), *[vmem] * (NX + 2), hbm],
        out_specs=hbm,
        scratch_shapes=[
            pltpu.VMEM((NX * FEAT * SAMP, E), F32),
            pltpu.VMEM((NX * SAMP, HID), BF),
            pltpu.VMEM((TIN, HID), BF),
            pltpu.SemaphoreType.DMA((UP_STEPS,)),
            pltpu.SemaphoreType.DMA((UP_STEPS, NX)),
        ],
        compiler_params=pltpu.CompilerParams(vmem_limit_bytes=32 << 20),
        cost_estimate=pl.CostEstimate(flops=5 << 30, bytes_accessed=20 << 20, transcendentals=0),
    )(me, grads, *hiddens, down, in_hbm(up))


def table_kernel(
    half,
    parts_ref,
    pooled_hbm_ref,
    out_ref,
    pooled_ref,
    pooled_sems,
    *scratch,
):
    table = Table(half, parts_ref, pooled_ref, out_ref, scratch)

    def pooled_copy(x):
        rows = pl.ds(x * FEAT * SAMP, FEAT * SAMP)
        return pltpu.make_async_copy(
            pooled_hbm_ref.at[rows], pooled_ref.at[rows], pooled_sems.at[x]
        )

    for x in range(NX):
        pooled_copy(x).start()
    table.begin()
    spilled = 0
    for x in range(NX):
        pooled_copy(x).wait()
        spilled = table.gather(x, spilled)
    table.finish(spilled)


def half_tables(half, parts, pooled):
    hbm = pl.BlockSpec(memory_space=pltpu.HBM)
    vmem = pl.BlockSpec(memory_space=pltpu.VMEM)
    return pl.pallas_call(
        functools.partial(table_kernel, half),
        out_shape=jax.ShapeDtypeStruct((NZ, HALF, E), BF),
        in_specs=[vmem, hbm],
        out_specs=vmem,
        scratch_shapes=[
            pltpu.VMEM((NX * FEAT * SAMP, E), F32),
            pltpu.SemaphoreType.DMA((NX,)),
            *TABLE_SCRATCH,
        ],
        compiler_params=pltpu.CompilerParams(vmem_limit_bytes=32 << 20),
        cost_estimate=pl.CostEstimate(flops=5 << 30, bytes_accessed=10 << 20, transcendentals=0),
    )(parts, in_hbm(pooled))


def local(
    out_grad,
    hidden_pre,
    down_proj,
    up_proj,
    feature_slot,
    element_segment,
    element_weight,
    row_owner,
    row_local,
):
    own = hidden_pre[0]
    near, side, far = [
        lax.ppermute(own, "x", [(i, i ^ r) for i in range(NX)]) for r in (1, 3, 2)
    ]
    hiddens = (own, near, far, side)
    by_tower = jnp.transpose(out_grad, (1, 0, 2))
    grads = lax.all_to_all(
        jnp.broadcast_to(by_tower, (NX, *by_tower.shape)).reshape(-1, *by_tower.shape[1:]),
        ("x", "tower"),
        split_axis=0,
        concat_axis=0,
        tiled=True,
    ).reshape(NX, SAMP, TOUT)
    swap_x = functools.partial(
        lax.all_to_all, axis_name="x", split_axis=0, concat_axis=0, tiled=True
    )
    flat = (1, ELEMS)
    buckets = bucket_elements(
        element_segment.reshape(flat),
        element_weight.reshape(flat),
        row_owner.reshape(flat),
        row_local.reshape(flat),
        feature_slot,
        grads,
    )
    parts = swap_x(buckets).reshape(NX, PIECES, CHUNKS * BUCKETS, LANES)
    me = lax.axis_index("x").astype(I32).reshape(1)
    pooled = pooled_gradients(me, grads, hiddens, down_proj[0], up_proj[0])
    swap = functools.partial(
        lax.all_to_all, axis_name="z", split_axis=0, concat_axis=0, tiled=True
    )
    first = swap(half_tables(0, parts, pooled))
    second = swap(half_tables(1, parts, pooled))
    table_grad = jnp.concatenate(
        [jnp.sum(first.astype(F32), axis=0), jnp.sum(second.astype(F32), axis=0)], axis=0
    )
    return table_grad.reshape(1, ROW_DEV, E)


def solution(mesh):
    towers = mesh.shape["tower"]
    grid = Mesh(mesh.devices.reshape(towers, NZ, NX), ("tower", "z", "x"))
    shard = ("z", "x")
    in_specs = (
        P(("tower", "z", "x"), None, None),
        P("tower", shard, None),
        P("tower", None, None),
        P("tower", None, None),
        P("tower", None),
        P("tower", shard, None),
        P("tower", shard, None),
        P("tower", shard, None, None),
        P("tower", shard, None),
    )
    out_specs = P("tower", shard, None)
    return jax.shard_map(local, mesh=grid, in_specs=in_specs, out_specs=out_specs, check_vma=False)
```

```python
import functools

import jax
import jax.numpy as jnp
from jax import lax
from jax.experimental import pallas as pl
from jax.experimental.pallas import tpu as pltpu
from jax.sharding import Mesh
from jax.sharding import PartitionSpec as P

E = 128
FEAT = 32
SAMP = 128
HID = 1024
TOUT = 256
TIN = 4096
ROW_DEV = 512
ELEMS = 5120
CAP = 320
NX = 4
NZ = 8
HALVES = 2
HALF = ROW_DEV // HALVES
BUCKETS = NZ * HALVES
SUBS = NX * BUCKETS
PIECES = 5
SLOTS = 384
LANES = 128
CHUNKS = SLOTS // LANES
USED = 120
STEP = 512
UNROLL = 16
BATCH = 4
BF = jnp.bfloat16
F32 = jnp.float32
I32 = jnp.int32
NT = (((1,), (1,)), ((), ()))


def in_hbm(operand):
    return pltpu.with_memory_space_constraint(operand, pltpu.HBM)


def bucket_kernel(
    seg_ref,
    weight_ref,
    owner_ref,
    row_ref,
    slot_ref,
    after_ref,
    out_ref,
    acc_ref,
):
    del after_ref
    square = (FEAT, FEAT)
    diagonal = lax.broadcasted_iota(I32, square, 0) == lax.broadcasted_iota(I32, square, 1)
    slots = jnp.sum(
        jnp.where(diagonal, slot_ref[...].astype(F32), 0.0), axis=1, keepdims=True
    )
    upper = (
        lax.broadcasted_iota(I32, (STEP, STEP), 0) <= lax.broadcasted_iota(I32, (STEP, STEP), 1)
    ).astype(F32).astype(BF)
    sub_ids = lax.broadcasted_iota(I32, (SUBS, STEP), 0)
    feat_ids = lax.broadcasted_iota(I32, (FEAT, STEP), 0)
    most = (CHUNKS - 1) * LANES
    slot_ids = lax.broadcasted_iota(I32, (most, STEP), 0).astype(F32)
    acc_ref[...] = jnp.zeros_like(acc_ref)

    def step(k, carry, first=0, width=most):
        cols = pl.ds(pl.multiple_of(k * STEP, STEP), STEP)
        seg = seg_ref[:, cols]
        weight = weight_ref[:, cols]
        owner = owner_ref[:, cols]
        row = row_ref[:, cols]
        sub = (owner & 3) * BUCKETS + (row >> 8) * NZ + (owner >> 2)
        mine = sub_ids == sub
        ones = jnp.where(mine, 1.0, 0.0)
        inclusive = jnp.dot(ones.astype(BF), upper, preferred_element_type=F32) + carry
        rank = jnp.sum(ones * inclusive, axis=0, keepdims=True) - 1.0
        block = jnp.sum(
            jnp.where(feat_ids == (seg & 31), slots, 0.0), axis=0, keepdims=True
        )
        sample = (seg >> 5).astype(F32)
        row_next = ((row & 255) + 1).astype(F32)
        high = weight.astype(BF).astype(F32)
        rest = weight - high
        middle = rest.astype(BF).astype(F32)
        pieces = (block, sample, row_next, high, middle)
        left = jnp.concatenate([(ones * piece).astype(BF) for piece in pieces], axis=0)
        place = rank
        for c in range(1, CHUNKS):
            place = place + jnp.where(rank >= c * USED, float(LANES - USED), 0.0)
        right = jnp.where(slot_ids[:width] == place - first, 1.0, 0.0).astype(BF)
        acc_ref[:, first : first + width] += lax.dot_general(
            left, right, NT, preferred_element_type=F32
        )
        return inclusive[:, STEP - 1 : STEP]

    nothing = jnp.zeros((SUBS, 1), F32)
    count = lax.fori_loop(0, ELEMS // STEP, step, nothing, unroll=10)

    @pl.when(jnp.max(count) > (CHUNKS - 1) * USED)
    def _():
        last = functools.partial(step, first=most, width=LANES)
        lax.fori_loop(0, ELEMS // STEP, last, nothing)

    count = jnp.broadcast_to(count.astype(I32), (SUBS, LANES))
    count_parts = ((count >> 7).astype(F32), (count & 127).astype(F32))
    spare = lax.broadcasted_iota(I32, (SUBS, LANES), 1) >= USED
    for p in range(PIECES):
        for c in range(CHUNKS):
            part = acc_ref[p * SUBS : (p + 1) * SUBS, c * LANES : (c + 1) * LANES]
            if p < 2 and c == 0:
                part = jnp.where(spare, count_parts[p], part)
            part = part.astype(BF)
            for x in range(NX):
                out_ref[x, p, c] = part[x * BUCKETS : (x + 1) * BUCKETS]


def bucket_elements(segment, weight, owner, row, slots, after):
    vmem = pl.BlockSpec(memory_space=pltpu.VMEM)
    operands = (segment, weight, owner, row, slots)
    return pl.pallas_call(
        bucket_kernel,
        out_shape=jax.ShapeDtypeStruct((NX, PIECES, CHUNKS, BUCKETS, LANES), BF),
        in_specs=[vmem] * 5 + [pl.BlockSpec(memory_space=pl.ANY)],
        out_specs=vmem,
        scratch_shapes=[pltpu.VMEM((PIECES * SUBS, SLOTS), F32)],
        compiler_params=pltpu.CompilerParams(vmem_limit_bytes=24 << 20),
        cost_estimate=pl.CostEstimate(flops=3 << 30, bytes_accessed=1 << 20, transcendentals=0),
    )(*[in_hbm(operand) for operand in operands], after)


def chosen(rows):
    row_ids = lax.broadcasted_iota(I32, (HALF, rows.shape[1]), 0) + 1
    return jnp.where(row_ids == rows, 1.0, 0.0).astype(BF)


TABLE_SCRATCH = (
    pltpu.VMEM((NZ * NX * LANES, E), F32),
    pltpu.VMEM((BATCH * LANES, E), F32),
    pltpu.VMEM((NZ, HALF, E), F32),
    pltpu.VMEM((NZ * NX * LANES, E), F32),
    pltpu.VMEM((NX * CHUNKS * BUCKETS, LANES), I32),
    pltpu.VMEM((NX * CHUNKS * BUCKETS, LANES), I32),
    pltpu.VMEM((NX * CHUNKS * BUCKETS, LANES), F32),
    pltpu.SMEM((CHUNKS * NX * NZ, LANES), I32),
    pltpu.SMEM((CHUNKS * NX * NZ,), I32),
    pltpu.SemaphoreType.DMA((CHUNKS, NX)),
)


class Table:
    def __init__(self, half, parts_ref, pooled_ref, out_ref, scratch):
        self.half = half
        self.parts_ref, self.pooled_ref, self.out_ref = parts_ref, pooled_ref, out_ref
        self.group_ref, self.spill_ref, self.total_ref, self.scale_ref = scratch[:4]
        self.place_ref, self.row_ref, self.weight_ref = scratch[4:7]
        self.index_ref, self.spilled_ref, self.index_sems = scratch[7:]

    def index_copy(self, c, x):
        start = (x * CHUNKS + c) * BUCKETS + self.half * NZ
        return pltpu.make_async_copy(
            self.place_ref.at[pl.ds(start, NZ)],
            self.index_ref.at[pl.ds((c * NX + x) * NZ, NZ)],
            self.index_sems.at[c, x],
        )

    def begin(self):
        for x in range(NX):
            block, sample, row, high, middle = [
                self.parts_ref[x, p].astype(F32) for p in range(PIECES)
            ]
            these = slice(x * CHUNKS * BUCKETS, (x + 1) * CHUNKS * BUCKETS)
            self.place_ref[these, :] = (block * SAMP + sample).astype(I32)
            self.row_ref[these, :] = row.astype(I32)
            self.weight_ref[these, :] = high + middle
        for c in range(CHUNKS):
            for x in range(NX):
                self.index_copy(c, x).start()
        self.group_ref[...] = jnp.zeros_like(self.group_ref)
        self.spill_ref[...] = jnp.zeros_like(self.spill_ref)
        blank = jnp.zeros((8 - NX, LANES), F32)
        for o in range(NZ):
            weights = [self.weight_ref[self.vector_row(0, x, o), :] for x in range(NX)]
            columns = jnp.concatenate([*weights, blank], axis=0).T
            for x in range(NX):
                start = (o * NX + x) * LANES
                self.scale_ref[start : start + LANES, :] = jnp.broadcast_to(
                    columns[:, x : x + 1], (LANES, E)
                )

    def vector_row(self, c, x, o):
        return pl.ds((x * CHUNKS + c) * BUCKETS + self.half * NZ + o, 1)

    def index_row(self, c, x, o):
        return (c * NX + x) * NZ + o

    def fetch(self, source_row, count, shift, target_ref, start):
        places = self.index_ref.at[source_row]

        def some(j, unused):
            source = j * UNROLL
            target = pl.multiple_of(start + j * UNROLL, UNROLL)
            for u in range(UNROLL):
                target_ref[pl.ds(target + u, 1), :] = self.pooled_ref[
                    pl.ds(places[source + u] + shift, 1), :
                ]
            return unused

        lax.fori_loop(0, (count + (UNROLL - 1)) // UNROLL, some, 0)

    def gather(self, x, spilled):
        self.index_copy(0, x).wait()

        def bucket_step(o, spilled):
            row = self.index_row(0, x, o)
            count = self.index_ref[row, USED]
            start = (o * NX + x) * LANES
            self.fetch(row, jnp.minimum(count, USED), x * (FEAT * SAMP), self.group_ref, start)
            for c in range(1, CHUNKS):
                self.spilled_ref[spilled] = (c * NZ + o) * NX + x
                spilled = spilled + (count > c * USED).astype(I32)
            return spilled

        return lax.fori_loop(0, NZ, bucket_step, spilled)

    def finish(self, spilled):
        for o in range(NZ):
            rows = jnp.concatenate(
                [self.row_ref[self.vector_row(0, x, o), :] for x in range(NX)], axis=1
            )
            these = slice(o * NX * LANES, (o + 1) * NX * LANES)
            values = (self.group_ref[these, :] * self.scale_ref[these, :]).astype(BF)
            self.total_ref[o] = jnp.dot(chosen(rows), values, preferred_element_type=F32)
        for c in range(1, CHUNKS):
            for x in range(NX):
                self.index_copy(c, x).wait()

        def spill_step(k, unused):
            entries = []
            for q in range(BATCH):
                number = k * BATCH + q
                entry = self.spilled_ref[jnp.minimum(number, spilled - 1)]
                x, o = entry & (NX - 1), (entry >> 2) & (NZ - 1)
                c = entry >> 5
                count = self.index_ref[self.index_row(0, x, o), USED] - c * USED
                count = jnp.where(number < spilled, jnp.minimum(count, USED), 0)
                shift = x * (FEAT * SAMP)
                self.fetch(self.index_row(c, x, o), count, shift, self.spill_ref, q * LANES)
                entries.append((x, o, c, count))
            for q, (x, o, c, count) in enumerate(entries):
                row = self.vector_row(c, x, o)
                weight = jnp.where(count > 0, self.weight_ref[row, :], 0.0)
                column = jnp.broadcast_to(weight, (8, LANES)).T[:, :1]
                values = self.spill_ref[q * LANES : (q + 1) * LANES, :] * column
                self.total_ref[o] += jnp.dot(
                    chosen(self.row_ref[row, :]),
                    values.astype(BF),
                    preferred_element_type=F32,
                )
            return unused

        lax.fori_loop(0, (spilled + (BATCH - 1)) // BATCH, spill_step, 0)
        self.out_ref[...] = self.total_ref[...].astype(BF)


UP_STEP = 1024
UP_STEPS = TIN // UP_STEP
UP_PART = 512


def backward_kernel(grad_ref, down_ref, backward_ref):
    backward_ref[...] = lax.dot_general(
        grad_ref[...], down_ref[...], NT, preferred_element_type=F32
    ).astype(BF)


def hidden_gradients(grads, down):
    vmem = pl.BlockSpec(memory_space=pltpu.VMEM)
    return pl.pallas_call(
        backward_kernel,
        out_shape=jax.ShapeDtypeStruct((NX * SAMP, HID), BF),
        in_specs=[vmem, vmem],
        out_specs=vmem,
        compiler_params=pltpu.CompilerParams(vmem_limit_bytes=16 << 20),
        cost_estimate=pl.CostEstimate(flops=1 << 28, bytes_accessed=2 << 20, transcendentals=0),
    )(grads.reshape(NX * SAMP, TOUT), down)


def pooled_kernel(
    me_ref,
    backward_ref,
    hidden0_ref,
    hidden1_ref,
    hidden2_ref,
    hidden3_ref,
    up_hbm_ref,
    pooled_hbm_ref,
    pooled_ref,
    hid_ref,
    up_ref,
    up_sems,
    pooled_sems,
):
    def up_copy(k):
        rows = pl.ds(pl.multiple_of(k * UP_STEP, UP_STEP), UP_STEP)
        return pltpu.make_async_copy(up_hbm_ref.at[rows], up_ref.at[rows], up_sems.at[k])

    def pooled_copy(k, x):
        start = x * FEAT * SAMP + k * UP_STEP // E * SAMP
        rows = pl.ds(pl.multiple_of(start, UP_STEP), UP_STEP)
        return pltpu.make_async_copy(
            pooled_ref.at[rows], pooled_hbm_ref.at[rows], pooled_sems.at[k, x]
        )

    for k in range(UP_STEPS):
        up_copy(k).start()
    for r, hidden_ref in enumerate((hidden0_ref, hidden1_ref, hidden2_ref, hidden3_ref)):
        there = pl.ds(pl.multiple_of((me_ref[0] ^ r) * SAMP, SAMP), SAMP)
        keep = hidden_ref[...].astype(F32) > 0
        backward = backward_ref[there, :].astype(F32)
        hid_ref[there, :] = jnp.where(keep, backward, 0.0).astype(BF)

    def up_step(k, unused):
        up_copy(k).wait()
        for j in range(UP_STEP // UP_PART):
            rows = pl.ds(pl.multiple_of(k * UP_STEP + j * UP_PART, UP_PART), UP_PART)
            result = lax.dot_general(
                hid_ref[...], up_ref[rows, :], NT, preferred_element_type=F32
            )
            result = result.astype(BF).astype(F32)
            for x in range(NX):
                for i in range(UP_PART // E):
                    block = (k * UP_STEP + j * UP_PART) // E + i
                    start = pl.multiple_of((x * FEAT + block) * SAMP, SAMP)
                    pooled_ref[pl.ds(start, SAMP), :] = result[
                        x * SAMP : (x + 1) * SAMP, i * E : (i + 1) * E
                    ]
        for x in range(NX):
            pooled_copy(k, x).start()
        return unused

    lax.fori_loop(0, UP_STEPS, up_step, 0)
    for k in range(UP_STEPS):
        for x in range(NX):
            pooled_copy(k, x).wait()


def pooled_gradients(me, backward, hiddens, up):
    hbm = pl.BlockSpec(memory_space=pltpu.HBM)
    vmem = pl.BlockSpec(memory_space=pltpu.VMEM)
    return pl.pallas_call(
        pooled_kernel,
        out_shape=pltpu.HBM((NX * FEAT * SAMP, E), F32),
        in_specs=[pl.BlockSpec(memory_space=pltpu.SMEM), *[vmem] * (NX + 1), hbm],
        out_specs=hbm,
        scratch_shapes=[
            pltpu.VMEM((NX * FEAT * SAMP, E), F32),
            pltpu.VMEM((NX * SAMP, HID), BF),
            pltpu.VMEM((TIN, HID), BF),
            pltpu.SemaphoreType.DMA((UP_STEPS,)),
            pltpu.SemaphoreType.DMA((UP_STEPS, NX)),
        ],
        compiler_params=pltpu.CompilerParams(vmem_limit_bytes=32 << 20),
        cost_estimate=pl.CostEstimate(flops=5 << 30, bytes_accessed=20 << 20, transcendentals=0),
    )(me, backward, *hiddens, in_hbm(up))


def table_kernel(
    half,
    parts_ref,
    pooled_hbm_ref,
    out_ref,
    pooled_ref,
    pooled_sems,
    *scratch,
):
    table = Table(half, parts_ref, pooled_ref, out_ref, scratch)

    def pooled_copy(x):
        rows = pl.ds(x * FEAT * SAMP, FEAT * SAMP)
        return pltpu.make_async_copy(
            pooled_hbm_ref.at[rows], pooled_ref.at[rows], pooled_sems.at[x]
        )

    for x in range(NX):
        pooled_copy(x).start()
    table.begin()
    spilled = 0
    for x in range(NX):
        pooled_copy(x).wait()
        spilled = table.gather(x, spilled)
    table.finish(spilled)


def half_tables(half, parts, pooled):
    hbm = pl.BlockSpec(memory_space=pltpu.HBM)
    vmem = pl.BlockSpec(memory_space=pltpu.VMEM)
    return pl.pallas_call(
        functools.partial(table_kernel, half),
        out_shape=jax.ShapeDtypeStruct((NZ, HALF, E), BF),
        in_specs=[vmem, hbm],
        out_specs=vmem,
        scratch_shapes=[
            pltpu.VMEM((NX * FEAT * SAMP, E), F32),
            pltpu.SemaphoreType.DMA((NX,)),
            *TABLE_SCRATCH,
        ],
        compiler_params=pltpu.CompilerParams(vmem_limit_bytes=32 << 20),
        cost_estimate=pl.CostEstimate(flops=5 << 30, bytes_accessed=10 << 20, transcendentals=0),
    )(parts, in_hbm(pooled))


def local(
    out_grad,
    hidden_pre,
    down_proj,
    up_proj,
    feature_slot,
    element_segment,
    element_weight,
    row_owner,
    row_local,
):
    own = hidden_pre[0]
    near, side, far = [
        lax.ppermute(own, "x", [(i, i ^ r) for i in range(NX)]) for r in (1, 3, 2)
    ]
    hiddens = (own, near, far, side)
    by_tower = jnp.transpose(out_grad, (1, 0, 2))
    grads = lax.all_to_all(
        jnp.broadcast_to(by_tower, (NX, *by_tower.shape)).reshape(-1, *by_tower.shape[1:]),
        ("x", "tower"),
        split_axis=0,
        concat_axis=0,
        tiled=True,
    ).reshape(NX, SAMP, TOUT)
    swap_x = functools.partial(
        lax.all_to_all, axis_name="x", split_axis=0, concat_axis=0, tiled=True
    )
    flat = (1, ELEMS)
    buckets = bucket_elements(
        element_segment.reshape(flat),
        element_weight.reshape(flat),
        row_owner.reshape(flat),
        row_local.reshape(flat),
        feature_slot,
        grads,
    )
    parts = swap_x(buckets).reshape(NX, PIECES, CHUNKS * BUCKETS, LANES)
    me = lax.axis_index("x").astype(I32).reshape(1)
    backward = hidden_gradients(grads, down_proj[0])
    pooled = pooled_gradients(me, backward, hiddens, up_proj[0])
    swap = functools.partial(
        lax.all_to_all, axis_name="z", split_axis=0, concat_axis=0, tiled=True
    )
    first = swap(half_tables(0, parts, pooled))
    second = swap(half_tables(1, parts, pooled))
    table_grad = jnp.concatenate(
        [jnp.sum(first.astype(F32), axis=0), jnp.sum(second.astype(F32), axis=0)], axis=0
    )
    return table_grad.reshape(1, ROW_DEV, E)


def solution(mesh):
    towers = mesh.shape["tower"]
    grid = Mesh(mesh.devices.reshape(towers, NZ, NX), ("tower", "z", "x"))
    shard = ("z", "x")
    in_specs = (
        P(("tower", "z", "x"), None, None),
        P("tower", shard, None),
        P("tower", None, None),
        P("tower", None, None),
        P("tower", None),
        P("tower", shard, None),
        P("tower", shard, None),
        P("tower", shard, None, None),
        P("tower", shard, None),
    )
    out_specs = P("tower", shard, None)
    return jax.shard_map(local, mesh=grid, in_specs=in_specs, out_specs=out_specs, check_vma=False)
```

```python
import functools

import jax
import jax.numpy as jnp
from jax import lax
from jax.experimental import pallas as pl
from jax.experimental.pallas import tpu as pltpu
from jax.sharding import Mesh
from jax.sharding import PartitionSpec as P

E = 128
FEAT = 32
SAMP = 128
HID = 1024
TOUT = 256
TIN = 4096
ROW_DEV = 512
ELEMS = 5120
CAP = 320
NX = 4
NZ = 8
HALVES = 2
HALF = ROW_DEV // HALVES
BUCKETS = NZ * HALVES
SUBS = NX * BUCKETS
PIECES = 5
SLOTS = 384
LANES = 128
CHUNKS = SLOTS // LANES
USED = 120
STEP = 512
UNROLL = 16
BATCH = 4
BF = jnp.bfloat16
F32 = jnp.float32
I32 = jnp.int32
NT = (((1,), (1,)), ((), ()))


def in_hbm(operand):
    return pltpu.with_memory_space_constraint(operand, pltpu.HBM)


def bucket_kernel(
    seg_ref,
    weight_ref,
    owner_ref,
    row_ref,
    slot_ref,
    after_ref,
    out_ref,
    acc_ref,
):
    del after_ref
    square = (FEAT, FEAT)
    diagonal = lax.broadcasted_iota(I32, square, 0) == lax.broadcasted_iota(I32, square, 1)
    slots = jnp.sum(
        jnp.where(diagonal, slot_ref[...].astype(F32), 0.0), axis=1, keepdims=True
    )
    upper = (
        lax.broadcasted_iota(I32, (STEP, STEP), 0) <= lax.broadcasted_iota(I32, (STEP, STEP), 1)
    ).astype(F32).astype(BF)
    sub_ids = lax.broadcasted_iota(I32, (SUBS, STEP), 0)
    feat_ids = lax.broadcasted_iota(I32, (FEAT, STEP), 0)
    most = (CHUNKS - 1) * LANES
    slot_ids = lax.broadcasted_iota(I32, (most, STEP), 0).astype(F32)
    acc_ref[...] = jnp.zeros_like(acc_ref)

    def step(k, carry, first=0, width=most):
        cols = pl.ds(pl.multiple_of(k * STEP, STEP), STEP)
        seg = seg_ref[:, cols]
        weight = weight_ref[:, cols]
        owner = owner_ref[:, cols]
        row = row_ref[:, cols]
        sub = (owner & 3) * BUCKETS + (row >> 8) * NZ + (owner >> 2)
        mine = sub_ids == sub
        ones = jnp.where(mine, 1.0, 0.0)
        inclusive = jnp.dot(ones.astype(BF), upper, preferred_element_type=F32) + carry
        rank = jnp.sum(ones * inclusive, axis=0, keepdims=True) - 1.0
        block = jnp.sum(
            jnp.where(feat_ids == (seg & 31), slots, 0.0), axis=0, keepdims=True
        )
        sample = (seg >> 5).astype(F32)
        row_next = ((row & 255) + 1).astype(F32)
        high = weight.astype(BF).astype(F32)
        rest = weight - high
        middle = rest.astype(BF).astype(F32)
        pieces = (block, sample, row_next, high, middle)
        left = jnp.concatenate([(ones * piece).astype(BF) for piece in pieces], axis=0)
        place = rank
        for c in range(1, CHUNKS):
            place = place + jnp.where(rank >= c * USED, float(LANES - USED), 0.0)
        right = jnp.where(slot_ids[:width] == place - first, 1.0, 0.0).astype(BF)
        acc_ref[:, first : first + width] += lax.dot_general(
            left, right, NT, preferred_element_type=F32
        )
        return inclusive[:, STEP - 1 : STEP]

    nothing = jnp.zeros((SUBS, 1), F32)
    count = lax.fori_loop(0, ELEMS // STEP, step, nothing, unroll=10)

    @pl.when(jnp.max(count) > (CHUNKS - 1) * USED)
    def _():
        last = functools.partial(step, first=most, width=LANES)
        lax.fori_loop(0, ELEMS // STEP, last, nothing)

    count = jnp.broadcast_to(count.astype(I32), (SUBS, LANES))
    count_parts = ((count >> 7).astype(F32), (count & 127).astype(F32))
    spare = lax.broadcasted_iota(I32, (SUBS, LANES), 1) >= USED
    for p in range(PIECES):
        for c in range(CHUNKS):
            part = acc_ref[p * SUBS : (p + 1) * SUBS, c * LANES : (c + 1) * LANES]
            if p < 2 and c == 0:
                part = jnp.where(spare, count_parts[p], part)
            part = part.astype(BF)
            for x in range(NX):
                out_ref[x, p, c] = part[x * BUCKETS : (x + 1) * BUCKETS]


def bucket_elements(segment, weight, owner, row, slots, after):
    vmem = pl.BlockSpec(memory_space=pltpu.VMEM)
    operands = (segment, weight, owner, row, slots)
    return pl.pallas_call(
        bucket_kernel,
        out_shape=jax.ShapeDtypeStruct((NX, PIECES, CHUNKS, BUCKETS, LANES), BF),
        in_specs=[vmem] * 5 + [pl.BlockSpec(memory_space=pl.ANY)],
        out_specs=vmem,
        scratch_shapes=[pltpu.VMEM((PIECES * SUBS, SLOTS), F32)],
        compiler_params=pltpu.CompilerParams(vmem_limit_bytes=24 << 20),
        cost_estimate=pl.CostEstimate(flops=3 << 30, bytes_accessed=1 << 20, transcendentals=0),
    )(*[in_hbm(operand) for operand in operands], after)


def chosen(rows):
    row_ids = lax.broadcasted_iota(I32, (HALF, rows.shape[1]), 0) + 1
    return jnp.where(row_ids == rows, 1.0, 0.0).astype(BF)


TABLE_SCRATCH = (
    pltpu.VMEM((NZ * NX * LANES, E), F32),
    pltpu.VMEM((BATCH * LANES, E), F32),
    pltpu.VMEM((NZ, HALF, E), F32),
    pltpu.VMEM((NZ * NX * LANES, E), F32),
    pltpu.VMEM((NX * CHUNKS * BUCKETS, LANES), I32),
    pltpu.VMEM((NX * CHUNKS * BUCKETS, LANES), I32),
    pltpu.VMEM((NX * CHUNKS * BUCKETS, LANES), F32),
    pltpu.SMEM((CHUNKS * NX * NZ, LANES), I32),
    pltpu.SMEM((CHUNKS * NX * NZ,), I32),
    pltpu.SemaphoreType.DMA((CHUNKS, NX)),
)


class Table:
    def __init__(self, half, parts_ref, pooled_ref, out_ref, scratch):
        self.half = half
        self.parts_ref, self.pooled_ref, self.out_ref = parts_ref, pooled_ref, out_ref
        self.group_ref, self.spill_ref, self.total_ref, self.scale_ref = scratch[:4]
        self.place_ref, self.row_ref, self.weight_ref = scratch[4:7]
        self.index_ref, self.spilled_ref, self.index_sems = scratch[7:]

    def index_copy(self, c, x):
        start = (x * CHUNKS + c) * BUCKETS + self.half * NZ
        return pltpu.make_async_copy(
            self.place_ref.at[pl.ds(start, NZ)],
            self.index_ref.at[pl.ds((c * NX + x) * NZ, NZ)],
            self.index_sems.at[c, x],
        )

    def begin(self):
        for x in range(NX):
            block, sample, row, high, middle = [
                self.parts_ref[x, p].astype(F32) for p in range(PIECES)
            ]
            these = slice(x * CHUNKS * BUCKETS, (x + 1) * CHUNKS * BUCKETS)
            self.place_ref[these, :] = (block * SAMP + sample).astype(I32)
            self.row_ref[these, :] = row.astype(I32)
            self.weight_ref[these, :] = high + middle
        for c in range(CHUNKS):
            for x in range(NX):
                self.index_copy(c, x).start()
        self.group_ref[...] = jnp.zeros_like(self.group_ref)
        self.spill_ref[...] = jnp.zeros_like(self.spill_ref)
        blank = jnp.zeros((8 - NX, LANES), F32)
        for o in range(NZ):
            weights = [self.weight_ref[self.vector_row(0, x, o), :] for x in range(NX)]
            columns = jnp.concatenate([*weights, blank], axis=0).T
            for x in range(NX):
                start = (o * NX + x) * LANES
                self.scale_ref[start : start + LANES, :] = jnp.broadcast_to(
                    columns[:, x : x + 1], (LANES, E)
                )

    def vector_row(self, c, x, o):
        return pl.ds((x * CHUNKS + c) * BUCKETS + self.half * NZ + o, 1)

    def index_row(self, c, x, o):
        return (c * NX + x) * NZ + o

    def fetch(self, source_row, count, shift, target_ref, start):
        places = self.index_ref.at[source_row]

        def some(j, unused):
            source = j * UNROLL
            target = pl.multiple_of(start + j * UNROLL, UNROLL)
            for u in range(UNROLL):
                target_ref[pl.ds(target + u, 1), :] = self.pooled_ref[
                    pl.ds(places[source + u] + shift, 1), :
                ]
            return unused

        lax.fori_loop(0, (count + (UNROLL - 1)) // UNROLL, some, 0)

    def gather(self, x, spilled):
        self.index_copy(0, x).wait()

        def bucket_step(o, spilled):
            row = self.index_row(0, x, o)
            count = self.index_ref[row, USED]
            start = (o * NX + x) * LANES
            self.fetch(row, jnp.minimum(count, USED), x * (FEAT * SAMP), self.group_ref, start)
            for c in range(1, CHUNKS):
                self.spilled_ref[spilled] = (c * NZ + o) * NX + x
                spilled = spilled + (count > c * USED).astype(I32)
            return spilled

        return lax.fori_loop(0, NZ, bucket_step, spilled)

    def finish(self, spilled):
        for o in range(NZ):
            rows = jnp.concatenate(
                [self.row_ref[self.vector_row(0, x, o), :] for x in range(NX)], axis=1
            )
            these = slice(o * NX * LANES, (o + 1) * NX * LANES)
            values = (self.group_ref[these, :] * self.scale_ref[these, :]).astype(BF)
            self.total_ref[o] = jnp.dot(chosen(rows), values, preferred_element_type=F32)
        for c in range(1, CHUNKS):
            for x in range(NX):
                self.index_copy(c, x).wait()

        def spill_step(k, unused):
            entries = []
            for q in range(BATCH):
                number = k * BATCH + q
                entry = self.spilled_ref[jnp.minimum(number, spilled - 1)]
                x, o = entry & (NX - 1), (entry >> 2) & (NZ - 1)
                c = entry >> 5
                count = self.index_ref[self.index_row(0, x, o), USED] - c * USED
                count = jnp.where(number < spilled, jnp.minimum(count, USED), 0)
                shift = x * (FEAT * SAMP)
                self.fetch(self.index_row(c, x, o), count, shift, self.spill_ref, q * LANES)
                entries.append((x, o, c, count))
            for q, (x, o, c, count) in enumerate(entries):
                row = self.vector_row(c, x, o)
                weight = jnp.where(count > 0, self.weight_ref[row, :], 0.0)
                column = jnp.broadcast_to(weight, (8, LANES)).T[:, :1]
                values = self.spill_ref[q * LANES : (q + 1) * LANES, :] * column
                self.total_ref[o] += jnp.dot(
                    chosen(self.row_ref[row, :]),
                    values.astype(BF),
                    preferred_element_type=F32,
                )
            return unused

        lax.fori_loop(0, (spilled + (BATCH - 1)) // BATCH, spill_step, 0)
        self.out_ref[...] = self.total_ref[...].astype(BF)


UP_STEP = 1024
UP_STEPS = TIN // UP_STEP
UP_PART = 512


def backward_kernel(grad_ref, down_ref, backward_ref):
    backward_ref[...] = lax.dot_general(
        grad_ref[...], down_ref[...], NT, preferred_element_type=F32
    ).astype(BF)


def hidden_gradients(grads, down):
    vmem = pl.BlockSpec(memory_space=pltpu.VMEM)
    return pl.pallas_call(
        backward_kernel,
        out_shape=jax.ShapeDtypeStruct((NX * SAMP, HID), BF),
        in_specs=[vmem, vmem],
        out_specs=vmem,
        compiler_params=pltpu.CompilerParams(vmem_limit_bytes=16 << 20),
        cost_estimate=pl.CostEstimate(flops=1 << 28, bytes_accessed=2 << 20, transcendentals=0),
    )(grads.reshape(NX * SAMP, TOUT), down)


def pooled_kernel(
    me_ref,
    backward_ref,
    hidden0_ref,
    hidden1_ref,
    hidden2_ref,
    hidden3_ref,
    up_hbm_ref,
    pooled_hbm_ref,
    pooled_ref,
    hid_ref,
    up_ref,
    up_sems,
    pooled_sems,
):
    def up_copy(k):
        rows = pl.ds(pl.multiple_of(k * UP_STEP, UP_STEP), UP_STEP)
        return pltpu.make_async_copy(up_hbm_ref.at[rows], up_ref.at[rows], up_sems.at[k])

    def pooled_copy(k, x):
        start = x * FEAT * SAMP + k * UP_STEP // E * SAMP
        rows = pl.ds(pl.multiple_of(start, UP_STEP), UP_STEP)
        return pltpu.make_async_copy(
            pooled_ref.at[rows], pooled_hbm_ref.at[rows], pooled_sems.at[k, x]
        )

    for k in range(UP_STEPS):
        up_copy(k).start()
    for r, hidden_ref in enumerate((hidden0_ref, hidden1_ref, hidden2_ref, hidden3_ref)):
        there = pl.ds(pl.multiple_of((me_ref[0] ^ r) * SAMP, SAMP), SAMP)
        keep = hidden_ref[...].astype(F32) > 0
        backward = backward_ref[there, :].astype(F32)
        hid_ref[there, :] = jnp.where(keep, backward, 0.0).astype(BF)

    def up_step(k, unused):
        up_copy(k).wait()
        for j in range(UP_STEP // UP_PART):
            rows = pl.ds(pl.multiple_of(k * UP_STEP + j * UP_PART, UP_PART), UP_PART)
            result = lax.dot_general(
                hid_ref[...], up_ref[rows, :], NT, preferred_element_type=F32
            )
            result = result.astype(BF).astype(F32)
            for x in range(NX):
                for i in range(UP_PART // E):
                    block = (k * UP_STEP + j * UP_PART) // E + i
                    start = pl.multiple_of((x * FEAT + block) * SAMP, SAMP)
                    pooled_ref[pl.ds(start, SAMP), :] = result[
                        x * SAMP : (x + 1) * SAMP, i * E : (i + 1) * E
                    ]
        for x in range(NX):
            pooled_copy(k, x).start()
        return unused

    lax.fori_loop(0, UP_STEPS, up_step, 0)
    for k in range(UP_STEPS):
        for x in range(NX):
            pooled_copy(k, x).wait()


def pooled_gradients(me, backward, hiddens, up):
    hbm = pl.BlockSpec(memory_space=pltpu.HBM)
    vmem = pl.BlockSpec(memory_space=pltpu.VMEM)
    return pl.pallas_call(
        pooled_kernel,
        out_shape=pltpu.HBM((NX * FEAT * SAMP, E), F32),
        in_specs=[pl.BlockSpec(memory_space=pltpu.SMEM), *[vmem] * (NX + 1), hbm],
        out_specs=hbm,
        scratch_shapes=[
            pltpu.VMEM((NX * FEAT * SAMP, E), F32),
            pltpu.VMEM((NX * SAMP, HID), BF),
            pltpu.VMEM((TIN, HID), BF),
            pltpu.SemaphoreType.DMA((UP_STEPS,)),
            pltpu.SemaphoreType.DMA((UP_STEPS, NX)),
        ],
        compiler_params=pltpu.CompilerParams(vmem_limit_bytes=32 << 20),
        cost_estimate=pl.CostEstimate(flops=5 << 30, bytes_accessed=20 << 20, transcendentals=0),
    )(me, backward, *hiddens, in_hbm(up))


def table_kernel(
    half,
    parts_ref,
    pooled_hbm_ref,
    out_ref,
    pooled_ref,
    pooled_sems,
    *scratch,
):
    table = Table(half, parts_ref, pooled_ref, out_ref, scratch)

    def pooled_copy(x):
        rows = pl.ds(x * FEAT * SAMP, FEAT * SAMP)
        return pltpu.make_async_copy(
            pooled_hbm_ref.at[rows], pooled_ref.at[rows], pooled_sems.at[x]
        )

    for x in range(NX):
        pooled_copy(x).start()
    table.begin()
    spilled = 0
    for x in range(NX):
        pooled_copy(x).wait()
        spilled = table.gather(x, spilled)
    table.finish(spilled)


def half_tables(half, parts, pooled):
    hbm = pl.BlockSpec(memory_space=pltpu.HBM)
    vmem = pl.BlockSpec(memory_space=pltpu.VMEM)
    return pl.pallas_call(
        functools.partial(table_kernel, half),
        out_shape=jax.ShapeDtypeStruct((NZ, HALF, E), BF),
        in_specs=[vmem, hbm],
        out_specs=vmem,
        scratch_shapes=[
            pltpu.VMEM((NX * FEAT * SAMP, E), F32),
            pltpu.SemaphoreType.DMA((NX,)),
            *TABLE_SCRATCH,
        ],
        compiler_params=pltpu.CompilerParams(vmem_limit_bytes=32 << 20),
        cost_estimate=pl.CostEstimate(flops=5 << 30, bytes_accessed=10 << 20, transcendentals=0),
    )(parts, in_hbm(pooled))


def local(
    out_grad,
    hidden_pre,
    down_proj,
    up_proj,
    feature_slot,
    element_segment,
    element_weight,
    row_owner,
    row_local,
):
    own = hidden_pre[0]
    near, side, far = [
        lax.ppermute(own, "x", [(i, i ^ r) for i in range(NX)]) for r in (1, 3, 2)
    ]
    hiddens = (own, near, far, side)
    by_tower = jnp.transpose(out_grad, (1, 0, 2))
    grads = lax.all_to_all(
        jnp.broadcast_to(by_tower, (NX, *by_tower.shape)).reshape(-1, *by_tower.shape[1:]),
        ("x", "tower"),
        split_axis=0,
        concat_axis=0,
        tiled=True,
    ).reshape(NX, SAMP, TOUT)
    swap_x = functools.partial(
        lax.all_to_all, axis_name="x", split_axis=0, concat_axis=0, tiled=True
    )
    flat = (1, ELEMS)
    buckets = bucket_elements(
        element_segment.reshape(flat),
        element_weight.reshape(flat),
        row_owner.reshape(flat),
        row_local.reshape(flat),
        feature_slot,
        grads,
    )
    parts = swap_x(buckets).reshape(NX, PIECES, CHUNKS * BUCKETS, LANES)
    me = lax.axis_index("x").astype(I32).reshape(1)
    backward = hidden_gradients(grads, down_proj[0])
    pooled = pooled_gradients(me, backward, hiddens, up_proj[0])
    swap = functools.partial(
        lax.all_to_all, axis_name="z", split_axis=0, concat_axis=0, tiled=True
    )
    first = swap(half_tables(0, parts, pooled))
    second = swap(half_tables(1, parts, pooled))
    table_grad = jnp.sum(jnp.concatenate([first, second], axis=1).astype(F32), axis=0)
    return table_grad.reshape(1, ROW_DEV, E)


def solution(mesh):
    towers = mesh.shape["tower"]
    grid = Mesh(mesh.devices.reshape(towers, NZ, NX), ("tower", "z", "x"))
    shard = ("z", "x")
    in_specs = (
        P(("tower", "z", "x"), None, None),
        P("tower", shard, None),
        P("tower", None, None),
        P("tower", None, None),
        P("tower", None),
        P("tower", shard, None),
        P("tower", shard, None),
        P("tower", shard, None, None),
        P("tower", shard, None),
    )
    out_specs = P("tower", shard, None)
    return jax.shard_map(local, mesh=grid, in_specs=in_specs, out_specs=out_specs, check_vma=False)
```
